32 devices in a mesh: group: 2 (over x), docs: 4 (over y, core), tensor: 4 (over z).
Axes of the slice: x: 2, y: 2, z: 4, core: 2. Of those that a mesh axis runs over, the one named last changes fastest.
Arguments:
- inputs: bfloat16 [8192, 8192], P(('group', 'docs'), 'tensor'), parts along dimension 0, may hold values from -6 to 6
- grads: bfloat16 [8192, 28672], P(('group', 'docs'), 'tensor'), parts along dimension 0, may hold values from -6 to 6
- proj_in: bfloat16 [8192, 64], P('tensor'), may hold values from -0.0625 to 0.0625
- proj_out: bfloat16 [28672, 64], P('tensor'), may hold values from -0.03125 to 0.03125
- queries: bfloat16 [4096, 4096], P(('group', 'docs'), 'tensor'), parts along dimension 0, may hold values from -3 to 3
- segment_ids: int32 [8, 1024], P(('group', 'docs')), parts along dimension 0, may hold values from 0 to 7, never falling along the last dimension, each value on 1 to 256 neighbouring positions
Outputs:
- scores: float32 [64, 4, 512], P(('group', 'docs'), None, 'tensor'), parts along dimension 0
The draws below stay inside these ranges and needn't reach their ends.
There are 2 independent parts, one for each index of `group`. The reference program is written for one: setup_inputs(seed, part) draws one part's arguments, and reference() takes and returns one part's arrays. A program takes and returns all parts, laid end to end along the dimension named above; an argument that names none is the same for every part. Nothing has to cross between parts.
Inputs may be any that keep to these rules, and one draw needn't show every extreme that they name: `segment_ids`: within each row the ids never fall, and each of the 8 ids names between 1 and 256 tokens, one exactly 256.
All inputs are finite; a program needn't handle non-finite values.
Results may differ from the reference program's by a relative error of at most 0.0029.
Values may be sent and summed in bfloat16 or wider, within the bound.
No kernel may reach another device: no remote copies, remote signals or barrier semaphores. Data moves between devices by JAX's collectives and lax.ppermute only.
A program may use at most 64 MiB of HBM per device.

```python
import math
import jax
import jax.numpy as jnp
import numpy as np
from jax import lax

D = 8192
FF = 28672
R = 64
TOK_DEV = 1024
DOC_DEV = 8
QROWS = 512
TOKENS = 4096
DOCS = 32
NQ = 2048
MOST = 256
N_DOCS = 4


def block_scale(stream_key, extent, shards, least, high):
    loudness = 1.0
    for axis_at, blocks in shards:
        draws = jax.random.uniform(jax.random.fold_in(jax.random.fold_in(stream_key, 6), axis_at), (blocks,), jnp.float32, least / len(shards), high / len(shards))
        loudness = loudness * jnp.repeat(jnp.exp(draws), extent[axis_at] // blocks).reshape((-1,) + (1,) * (len(extent) - 1 - axis_at))
    return loudness


def split_up(number_of, total, limit, lean):
    loads = [(1 << 20) // math.isqrt(grade ** lean) + 1 for grade in range(2, number_of + 1)]
    rest, given = total - limit - (number_of - 1), [1] * (number_of - 1)
    while rest > 0:
        free = [i for i in range(number_of - 1) if given[i] < limit]
        pool, budget = sum([loads[i] for i in free]), rest
        for i in free:
            more = min(limit - given[i], max(1, budget * loads[i] // pool), rest)
            given[i] = given[i] + more
            rest = rest - more
    return np.array([limit] + given)


def ragged(rng, count, total, bound, slope):
    if count == 2:
        one = jax.random.randint(rng, (), max(1, total - bound), min(bound, total - 1) + 1)
        return jnp.stack([one, total - one])
    lengths = jnp.asarray(split_up(count, total, bound, slope), jnp.int32)
    couples = (count - 1) // 2
    donor, receiver = lengths[1:1 + 2 * couples:2], lengths[2:2 + 2 * couples:2]
    slack = jnp.minimum(donor - 1, bound - receiver)
    moved = jax.random.randint(jax.random.fold_in(rng, 1), (couples,), 0, 1 << 20) % (slack + 1)
    lengths = lengths.at[1:1 + 2 * couples:2].set(donor - moved).at[2:2 + 2 * couples:2].set(receiver + moved)
    return lengths[jax.random.permutation(jax.random.fold_in(rng, 2), count)]


def noise(rng, shape, scale, most, cuts=(), held_as=jnp.bfloat16):
    values = scale * jax.random.normal(rng, shape, jnp.float32)
    if cuts:
        values = values * block_scale(rng, shape, cuts, -0.22, 0.18)
    return jnp.clip(values, -most, most).astype(held_as)


def setup_inputs(seed: int = 0, part: int = 0) -> dict:
    key_of = jax.random.split(jax.random.key(seed), 7)
    part_splits = jax.random.split(jax.random.fold_in(key_of[6], part), 7)
    inputs = noise(part_splits[0], (TOKENS, D), 1.0, 6.0, ((0, 4), (1, 4)))
    grads = noise(part_splits[1], (TOKENS, FF), 1.0, 6.0, ((0, 4), (1, 4)))
    proj_in = noise(key_of[2], (D, R), D ** -0.5, 0.0625, ((0, 4),))
    proj_out = noise(key_of[3], (FF, R), FF ** -0.5, 0.03125, ((0, 4),))
    queries = noise(part_splits[4], (NQ, R * R), 0.2, 3.0, ((0, 4), (1, 4)))
    segment_ids = jax.vmap(lambda own: jnp.searchsorted(jnp.cumsum(ragged(own, DOC_DEV, TOK_DEV, MOST, 1)), jnp.arange(TOK_DEV), side="right"))(jax.random.split(part_splits[5], N_DOCS)).reshape((N_DOCS, TOK_DEV)).astype(jnp.int32)
    return dict(inputs=inputs, grads=grads, proj_in=proj_in, proj_out=proj_out, queries=queries, segment_ids=segment_ids)


def reference(inputs, grads, proj_in, proj_out, queries, segment_ids):
    xp = jnp.dot(inputs, proj_in, preferred_element_type=jnp.float32)
    gp = jnp.dot(grads, proj_out, preferred_element_type=jnp.float32)
    xp_blocks = xp.reshape(N_DOCS, TOK_DEV, R)
    gp_blocks = gp.reshape(N_DOCS, TOK_DEV, R)

    def one_block(packed):
        ids, x_rows, g_rows = packed
        onehot = (ids[:, None] == jnp.arange(DOC_DEV, dtype=jnp.int32)[None, :]).astype(jnp.float32)
        counts = jnp.sum(onehot, axis=0)
        weighted = (onehot[:, :, None] * g_rows[:, None, :]).reshape(TOK_DEV, DOC_DEV * R)
        summed = jnp.dot(weighted.T, x_rows, precision=lax.Precision.HIGHEST)
        summed = summed.reshape(DOC_DEV, R * R)
        return (summed / counts[:, None]).astype(jnp.bfloat16)

    train = lax.map(one_block, (segment_ids, xp_blocks, gp_blocks)).reshape(DOCS, R * R)
    scores = jnp.dot(train, queries.T, preferred_element_type=jnp.float32)
    return scores.reshape(DOCS, N_DOCS, QROWS)
```

```python
import functools

import jax
import jax.numpy as jnp
from jax import lax
from jax.experimental import pallas as pl
from jax.experimental.pallas import tpu as pltpu
from jax.sharding import PartitionSpec as P

DOC_DEV = 8
F32 = jnp.float32
BF16 = jnp.bfloat16
NT = (((1,), (1,)), ((), ()))
VMEM = pl.BlockSpec(memory_space=pltpu.VMEM)
ANY = pl.BlockSpec(memory_space=pl.ANY)
PIECES = 2


def swapped(block, axis, flip):
    return lax.ppermute(block, axis, [(i, i ^ flip) for i in range(lax.axis_size(axis))])


def project_kernel(flips, x_hbm, g_hbm, px_hbm, pg_hbm, *rest):
    outs, (xb, gb, px, pg, sems, wsems) = rest[: len(flips)], rest[len(flips) :]
    me = lax.axis_index("tensor")
    rank, chunk = px.shape[0], xb.shape[1]
    kx, kg = xb.shape[2], gb.shape[2]
    total = len(flips) * PIECES

    def copies(p):
        row = pl.multiple_of((me ^ flips[p // PIECES]) * chunk, chunk)
        i = p % PIECES
        return (
            pltpu.make_async_copy(x_hbm.at[pl.ds(row, chunk), pl.ds(i * kx, kx)], xb.at[p], sems.at[0, p]),
            pltpu.make_async_copy(g_hbm.at[pl.ds(row, chunk), pl.ds(i * kg, kg)], gb.at[p], sems.at[1, p]),
        )

    weights = (
        pltpu.make_async_copy(px_hbm, px, wsems.at[0]),
        pltpu.make_async_copy(pg_hbm, pg, wsems.at[1]),
    )
    for c in weights:
        c.start()
    ahead = min(2, total)
    for p in range(ahead):
        for c in copies(p):
            c.start()
    for c in weights:
        c.wait()
    for p in range(total):
        i, out = p % PIECES, outs[p // PIECES]
        for c in copies(p):
            c.wait()
        if p + ahead < total:
            for c in copies(p + ahead):
                c.start()

        @pl.when(me >= 0)
        def _():
            dx = lax.dot_general(xb[p], px[:, i * kx : (i + 1) * kx], NT, preferred_element_type=F32).T
            dg = lax.dot_general(gb[p], pg[:, i * kg : (i + 1) * kg], NT, preferred_element_type=F32).T
            if i == 0:
                out[:rank, :] = dx
                out[rank:, :] = dg
            else:
                out[:rank, :] += dx
                out[rank:, :] += dg


def project(flips, inputs, grads, proj_in_t, proj_out_t, chunk):
    rank = proj_in_t.shape[0]
    total = len(flips) * PIECES
    kx, kg = inputs.shape[1] // PIECES, grads.shape[1] // PIECES
    return pl.pallas_call(
        functools.partial(project_kernel, flips),
        out_shape=[jax.ShapeDtypeStruct((2 * rank, chunk), F32)] * len(flips),
        in_specs=[ANY] * 4,
        out_specs=[VMEM] * len(flips),
        scratch_shapes=[
            pltpu.VMEM((total, chunk, kx), BF16),
            pltpu.VMEM((total, chunk, kg), BF16),
            pltpu.VMEM(proj_in_t.shape, BF16),
            pltpu.VMEM(proj_out_t.shape, BF16),
            pltpu.SemaphoreType.DMA((2, total)),
            pltpu.SemaphoreType.DMA((2,)),
        ],
        compiler_params=pltpu.CompilerParams(vmem_limit_bytes=32 * 2**20),
        name="project",
    )(inputs, grads, proj_in_t, proj_out_t)


def outer_kernel(shares, ids, *refs):
    parts, outs, (prod,) = refs[:shares], refs[shares : 2 * shares], refs[2 * shares :]
    me = lax.axis_index("tensor")
    rank, chunk = parts[0].shape[0] // 2, parts[0].shape[1]
    both = parts[0][...]
    for part in parts[1:]:
        both = both + part[...]
    x, g = both[:rank], both[rank:]
    own = ids[:, pl.ds(pl.multiple_of(me * chunk, chunk), chunk)]
    mask = own == lax.broadcasted_iota(jnp.int32, (DOC_DEV, chunk), 0)
    rows = jnp.concatenate([jnp.where(mask, g[i : i + 1], 0.0) for i in range(rank)], axis=0)
    rows_hi = rows.astype(BF16)
    rows_lo = (rows - rows_hi.astype(F32)).astype(BF16)
    x_hi = x.astype(BF16)
    x_lo = (x - x_hi.astype(F32)).astype(BF16)
    dot = functools.partial(lax.dot_general, dimension_numbers=NT, preferred_element_type=F32)
    total = dot(rows_hi, x_hi) + (dot(rows_hi, x_lo) + dot(rows_lo, x_hi))
    prod[...] = total.reshape(rank, DOC_DEV, rank)
    share = rank // shares
    for k in range(shares):
        first = (me ^ k) * share
        outs[k][...] = jnp.concatenate([prod[first + r] for r in range(share)], axis=1)


def outer(parts, ids):
    shares = len(parts)
    rank = parts[0].shape[0] // 2
    return pl.pallas_call(
        functools.partial(outer_kernel, shares),
        out_shape=[jax.ShapeDtypeStruct((DOC_DEV, rank * rank // shares), F32)] * shares,
        in_specs=[VMEM] * (1 + shares),
        out_specs=[VMEM] * shares,
        scratch_shapes=[pltpu.VMEM((rank, DOC_DEV, rank), F32)],
        name="outer",
    )(ids, *parts)


def train_kernel(ids, *refs):
    parts, out = refs[:-1], refs[-1]
    total = parts[0][...]
    for part in parts[1:]:
        total = total + part[...]
    hits = ids[...] == lax.broadcasted_iota(jnp.int32, (DOC_DEV, ids.shape[1]), 0)
    counts = jnp.sum(hits.astype(F32), axis=1, keepdims=True)
    train = total / counts
    half = train.shape[1] // 2
    out[...] = jnp.concatenate([train[:, :half], train[:, half:]], axis=0).astype(BF16)


def mean_gradients(parts, ids):
    width = parts[0].shape[1]
    return pl.pallas_call(
        train_kernel,
        out_shape=jax.ShapeDtypeStruct((2 * DOC_DEV, width // 2), BF16),
        in_specs=[VMEM] * (1 + len(parts)),
        out_specs=VMEM,
        name="train",
    )(ids, *parts)


def score_kernel(shares, near, far, *refs):
    trains, outs, (held,) = refs[: -shares - 1], refs[-shares - 1 : -1], refs[-1:]
    me = lax.axis_index("tensor")
    rows = []
    for train in trains:
        t = train[...].astype(F32)
        rows.append(jnp.concatenate([t[:DOC_DEV], t[DOC_DEV:]], axis=1))
    docs = jnp.concatenate(rows, axis=0).astype(BF16)
    count = docs.shape[0]
    width = near.shape[0] // shares
    for at, queries in enumerate((near, far)):
        scores = lax.dot_general(docs, queries[...], NT, preferred_element_type=F32)
        for j in range(shares):
            held[j, at * count : (at + 1) * count, :] = scores[:, j * width : (j + 1) * width]
    for k in range(shares):
        outs[k][...] = held[me ^ k]


def score(trains, near, far, shares):
    shape = (2 * DOC_DEV * len(trains), near.shape[0] // shares)
    return pl.pallas_call(
        functools.partial(score_kernel, shares),
        out_shape=[jax.ShapeDtypeStruct(shape, F32)] * shares,
        in_specs=[VMEM] * (2 + len(trains)),
        out_specs=[VMEM] * shares,
        scratch_shapes=[pltpu.VMEM((shares, *shape), F32)],
        name="score",
    )(near, far, *trains)


def add_kernel(shares, *refs):
    parts, outs = refs[:shares], refs[shares:]
    total = parts[0][...]
    for part in parts[1:]:
        total = total + part[...]
    count = total.shape[0] // 2
    for m, out in enumerate(outs):
        a = m * DOC_DEV
        out[...] = jnp.concatenate([total[a : a + DOC_DEV], total[count + a : count + a + DOC_DEV]], axis=0)


def add(parts, chips):
    return pl.pallas_call(
        functools.partial(add_kernel, len(parts)),
        out_shape=[jax.ShapeDtypeStruct((2 * DOC_DEV, parts[0].shape[1]), F32)] * chips,
        in_specs=[VMEM] * len(parts),
        out_specs=[VMEM] * chips,
        name="add",
    )(*parts)


def place_kernel(*refs):
    parts, out = refs[:-1], refs[-1]
    me = lax.axis_index("docs")
    for m, part in enumerate(parts):
        block = me ^ (2 * m)
        out[:, pl.ds(block, 1), :] = part[:DOC_DEV, :][:, None, :]
        out[:, pl.ds(block ^ 1, 1), :] = part[DOC_DEV:, :][:, None, :]


def place(parts):
    return pl.pallas_call(
        place_kernel,
        out_shape=jax.ShapeDtypeStruct((DOC_DEV, 2 * len(parts), parts[0].shape[1]), F32),
        in_specs=[VMEM] * len(parts),
        out_specs=VMEM,
        name="place",
    )(*parts)


def per_device(inputs, grads, proj_in, proj_out, queries, ids):
    shares, ndev = lax.axis_size("tensor"), lax.axis_size("docs")
    chips = ndev // 2
    chunk = inputs.shape[0] // shares
    sibling = swapped(queries, "docs", 1)
    flips = list(range(shares - 1, 0, -1))
    parts = project(flips, inputs, grads, proj_in.T, proj_out.T, chunk)
    arrived = [swapped(p, "tensor", k) for k, p in zip(flips, parts)]
    (own,) = project([0], inputs, grads, proj_in.T, proj_out.T, chunk)
    sums = outer([own] + arrived, ids)
    arrived = [swapped(sums[k], "tensor", k) for k in flips]
    train = mean_gradients([sums[0]] + arrived, ids)
    trains = [train] + [swapped(train, "docs", 2 * m) for m in range(1, chips)]
    scores = score(trains, queries, sibling, shares)
    arrived = [swapped(scores[k], "tensor", k) for k in flips]
    mine = add([scores[0]] + arrived, chips)
    return place([mine[0]] + [swapped(mine[m], "docs", 2 * m) for m in range(1, chips)])


def solution(mesh):
    in_specs = (
        P(("group", "docs"), "tensor"),
        P(("group", "docs"), "tensor"),
        P("tensor", None),
        P("tensor", None),
        P(("group", "docs"), "tensor"),
        P(("group", "docs"), None),
    )
    out_specs = P(("group", "docs"), None, "tensor")
    return jax.shard_map(
        per_device, mesh=mesh, in_specs=in_specs, out_specs=out_specs, check_vma=False
    )
```

```python
import functools

import jax
import jax.numpy as jnp
from jax import lax
from jax.experimental import pallas as pl
from jax.experimental.pallas import tpu as pltpu
from jax.sharding import PartitionSpec as P

DOC_DEV = 8
F32 = jnp.float32
BF16 = jnp.bfloat16
NT = (((1,), (1,)), ((), ()))
VMEM = pl.BlockSpec(memory_space=pltpu.VMEM)
HBM = pl.BlockSpec(memory_space=pltpu.HBM)
SMALL = pltpu.CompilerParams(vmem_limit_bytes=8 * 2**20)
PIECES = 2
STEPS = 32000.0
TAIL = 16


def swapped(block, axis, flip):
    return lax.ppermute(block, axis, [(i, i ^ flip) for i in range(lax.axis_size(axis))])


def encode(out, dx, dg):
    rank, chunk = dx.shape
    exponents = []
    for at, v in ((0, dx), (rank, dg)):
        top = jnp.maximum(jnp.max(jnp.abs(v), axis=0, keepdims=True), 1e-30)
        e = jnp.floor(jnp.log2(top)) + 1.0
        scaled = jnp.clip(jnp.round(v * (jnp.exp2(-e) * STEPS)), -32767.0, 32767.0)
        out[at : at + rank, :] = scaled.astype(jnp.int32).astype(jnp.int16)
        exponents.append(e.astype(jnp.int32))
    row = lax.broadcasted_iota(jnp.int32, (TAIL, chunk), 0)
    out[2 * rank :, :] = jnp.where(row == 0, exponents[0], jnp.where(row == 1, exponents[1], 0)).astype(jnp.int16)


def decode(part, rank):
    v = part[...].astype(jnp.int32).astype(F32)
    unit = jnp.exp2(v[2 * rank : 2 * rank + 2]) * (1.0 / STEPS)
    return v[:rank] * unit[0:1], v[rank : 2 * rank] * unit[1:2]


def project_kernel(flips, x_hbm, g_hbm, px_hbm, pg_hbm, *rest):
    outs, (xb, gb, px, pg, accx, accg, sems, wsems) = rest[: len(flips)], rest[len(flips) :]
    me = lax.axis_index("tensor")
    rank, chunk = px.shape[0], xb.shape[1]
    kx, kg = xb.shape[2], gb.shape[2]
    total = len(flips) * PIECES

    def copies(p):
        row = pl.multiple_of((me ^ flips[p // PIECES]) * chunk, chunk)
        i = p % PIECES
        return (
            pltpu.make_async_copy(x_hbm.at[pl.ds(row, chunk), pl.ds(i * kx, kx)], xb.at[p], sems.at[0, p]),
            pltpu.make_async_copy(g_hbm.at[pl.ds(row, chunk), pl.ds(i * kg, kg)], gb.at[p], sems.at[1, p]),
        )

    weights = (
        pltpu.make_async_copy(px_hbm, px, wsems.at[0]),
        pltpu.make_async_copy(pg_hbm, pg, wsems.at[1]),
    )
    for c in weights:
        c.start()
    ahead = min(2, total)
    for p in range(ahead):
        for c in copies(p):
            c.start()
    for c in weights:
        c.wait()
    for p in range(total):
        i, out = p % PIECES, outs[p // PIECES]
        for c in copies(p):
            c.wait()
        if p + ahead < total:
            for c in copies(p + ahead):
                c.start()

        @pl.when(me >= 0)
        def _():
            dx = lax.dot_general(xb[p], px[:, i * kx : (i + 1) * kx], NT, preferred_element_type=F32)
            dg = lax.dot_general(gb[p], pg[:, i * kg : (i + 1) * kg], NT, preferred_element_type=F32)
            if i > 0:
                dx, dg = dx + accx[...], dg + accg[...]
            if i < PIECES - 1:
                accx[...], accg[...] = dx, dg
            else:
                dx, dg = dx.T, dg.T
                if flips[p // PIECES]:
                    encode(out, dx, dg)
                else:
                    out[:rank, :], out[rank:, :] = dx, dg


def project(flips, inputs, grads, proj_in_t, proj_out_t, chunk):
    rank = proj_in_t.shape[0]
    total = len(flips) * PIECES
    kx, kg = inputs.shape[1] // PIECES, grads.shape[1] // PIECES
    return pl.pallas_call(
        functools.partial(project_kernel, flips),
        out_shape=[
            jax.ShapeDtypeStruct((2 * rank + TAIL, chunk), jnp.int16)
            if k
            else jax.ShapeDtypeStruct((2 * rank, chunk), F32)
            for k in flips
        ],
        in_specs=[HBM] * 4,
        out_specs=[VMEM] * len(flips),
        scratch_shapes=[
            pltpu.VMEM((total, chunk, kx), BF16),
            pltpu.VMEM((total, chunk, kg), BF16),
            pltpu.VMEM(proj_in_t.shape, BF16),
            pltpu.VMEM(proj_out_t.shape, BF16),
            pltpu.VMEM((chunk, rank), F32),
            pltpu.VMEM((chunk, rank), F32),
            pltpu.SemaphoreType.DMA((2, total)),
            pltpu.SemaphoreType.DMA((2,)),
        ],
        compiler_params=pltpu.CompilerParams(vmem_limit_bytes=60 * 2**20),
        name="project",
    )(inputs, grads, proj_in_t, proj_out_t)


def outer_kernel(shares, ids, *refs):
    parts, outs, (prod,) = refs[:shares], refs[shares : 2 * shares], refs[2 * shares :]
    me = lax.axis_index("tensor")
    rank, chunk = parts[0].shape[0] // 2, parts[0].shape[1]
    x, g = parts[0][:rank], parts[0][rank:]
    for part in parts[1:]:
        more_x, more_g = decode(part, rank)
        x, g = x + more_x, g + more_g
    own = ids[:, pl.ds(pl.multiple_of(me * chunk, chunk), chunk)]
    mask = own == lax.broadcasted_iota(jnp.int32, (DOC_DEV, chunk), 0)
    rows = jnp.concatenate([jnp.where(mask, g[i : i + 1], 0.0) for i in range(rank)], axis=0)
    rows_hi = rows.astype(BF16)
    rows_lo = (rows - rows_hi.astype(F32)).astype(BF16)
    x_hi = x.astype(BF16)
    x_lo = (x - x_hi.astype(F32)).astype(BF16)
    dot = functools.partial(lax.dot_general, dimension_numbers=NT, preferred_element_type=F32)
    total = dot(rows_hi, x_hi) + (dot(rows_hi, x_lo) + dot(rows_lo, x_hi))
    prod[...] = total.reshape(rank, DOC_DEV, rank)
    share = rank // shares
    for k in range(shares):
        first = (me ^ k) * share
        outs[k][...] = jnp.concatenate([prod[first + r] for r in range(share)], axis=1)


def outer(parts, ids):
    shares = len(parts)
    rank = parts[0].shape[0] // 2
    return pl.pallas_call(
        functools.partial(outer_kernel, shares),
        out_shape=[jax.ShapeDtypeStruct((DOC_DEV, rank * rank // shares), F32)] * shares,
        in_specs=[VMEM] * (1 + shares),
        out_specs=[VMEM] * shares,
        scratch_shapes=[pltpu.VMEM((rank, DOC_DEV, rank), F32)],
        compiler_params=SMALL,
        name="outer",
    )(ids, *parts)


def train_kernel(ids, *refs):
    parts, out = refs[:-1], refs[-1]
    total = parts[0][...]
    for part in parts[1:]:
        total = total + part[...]
    hits = ids[...] == lax.broadcasted_iota(jnp.int32, (DOC_DEV, ids.shape[1]), 0)
    counts = jnp.sum(hits.astype(F32), axis=1, keepdims=True)
    train = total / counts
    half = train.shape[1] // 2
    out[...] = jnp.concatenate([train[:, :half], train[:, half:]], axis=0).astype(BF16)


def mean_gradients(parts, ids):
    width = parts[0].shape[1]
    return pl.pallas_call(
        train_kernel,
        out_shape=jax.ShapeDtypeStruct((2 * DOC_DEV, width // 2), BF16),
        in_specs=[VMEM] * (1 + len(parts)),
        out_specs=VMEM,
        compiler_params=SMALL,
        name="train",
    )(ids, *parts)


def score_kernel(shares, near, far, *refs):
    trains, outs, (held,) = refs[: -shares - 1], refs[-shares - 1 : -1], refs[-1:]
    me = lax.axis_index("tensor")
    rows = []
    for train in trains:
        t = train[...].astype(F32)
        rows.append(jnp.concatenate([t[:DOC_DEV], t[DOC_DEV:]], axis=1))
    docs = jnp.concatenate(rows, axis=0).astype(BF16)
    count = docs.shape[0]
    width = near.shape[0] // shares
    for at, queries in enumerate((near, far)):
        scores = lax.dot_general(docs, queries[...], NT, preferred_element_type=F32)
        for j in range(shares):
            held[j, at * count : (at + 1) * count, :] = scores[:, j * width : (j + 1) * width]
    for k in range(shares):
        outs[k][...] = held[me ^ k]


def score(trains, near, far, shares):
    shape = (2 * DOC_DEV * len(trains), near.shape[0] // shares)
    return pl.pallas_call(
        functools.partial(score_kernel, shares),
        out_shape=[jax.ShapeDtypeStruct(shape, F32)] * shares,
        in_specs=[VMEM] * (2 + len(trains)),
        out_specs=[VMEM] * shares,
        scratch_shapes=[pltpu.VMEM((shares, *shape), F32)],
        compiler_params=SMALL,
        name="score",
    )(near, far, *trains)


def add_kernel(shares, *refs):
    parts, outs = refs[:shares], refs[shares:]
    total = parts[0][...]
    for part in parts[1:]:
        total = total + part[...]
    count = total.shape[0] // 2
    for m, out in enumerate(outs):
        a = m * DOC_DEV
        out[...] = jnp.concatenate([total[a : a + DOC_DEV], total[count + a : count + a + DOC_DEV]], axis=0)


def add(parts, chips):
    return pl.pallas_call(
        functools.partial(add_kernel, len(parts)),
        out_shape=[jax.ShapeDtypeStruct((2 * DOC_DEV, parts[0].shape[1]), F32)] * chips,
        in_specs=[VMEM] * len(parts),
        out_specs=[VMEM] * chips,
        compiler_params=SMALL,
        name="add",
    )(*parts)


def place_kernel(*refs):
    parts, out = refs[:-1], refs[-1]
    me = lax.axis_index("docs")
    for m, part in enumerate(parts):
        block = me ^ (2 * m)
        out[:, pl.ds(block, 1), :] = part[:DOC_DEV, :][:, None, :]
        out[:, pl.ds(block ^ 1, 1), :] = part[DOC_DEV:, :][:, None, :]


def place(parts):
    return pl.pallas_call(
        place_kernel,
        out_shape=jax.ShapeDtypeStruct((DOC_DEV, 2 * len(parts), parts[0].shape[1]), F32),
        in_specs=[VMEM] * len(parts),
        out_specs=VMEM,
        compiler_params=SMALL,
        name="place",
    )(*parts)


def groups_of(shares):
    flips = list(range(shares - 1, -1, -1))
    return [flips[:-1], flips[-1:]]


def per_device(inputs, grads, proj_in, proj_out, queries, ids):
    shares, ndev = lax.axis_size("tensor"), lax.axis_size("docs")
    chips = ndev // 2
    chunk = inputs.shape[0] // shares
    sibling = swapped(queries, "docs", 1)
    flips = list(range(shares - 1, 0, -1))
    parts = {}
    for group in groups_of(shares):
        made = project(group, inputs, grads, proj_in.T, proj_out.T, chunk)
        for k, part in zip(group, made):
            parts[k] = swapped(part, "tensor", k) if k else part
    sums = outer([parts[k] for k in range(shares)], ids)
    arrived = [swapped(sums[k], "tensor", k) for k in flips]
    train = mean_gradients([sums[0]] + arrived, ids)
    trains = [train] + [swapped(train, "docs", 2 * m) for m in range(1, chips)]
    scores = score(trains, queries, sibling, shares)
    arrived = [swapped(scores[k], "tensor", k) for k in flips]
    mine = add([scores[0]] + arrived, chips)
    return place([mine[0]] + [swapped(mine[m], "docs", 2 * m) for m in range(1, chips)])


def solution(mesh):
    in_specs = (
        P(("group", "docs"), "tensor"),
        P(("group", "docs"), "tensor"),
        P("tensor", None),
        P("tensor", None),
        P(("group", "docs"), "tensor"),
        P(("group", "docs"), None),
    )
    out_specs = P(("group", "docs"), None, "tensor")
    return jax.shard_map(
        per_device, mesh=mesh, in_specs=in_specs, out_specs=out_specs, check_vma=False
    )
```

```python
import functools

import jax
import jax.numpy as jnp
from jax import lax
from jax.experimental import pallas as pl
from jax.experimental.pallas import tpu as pltpu
from jax.sharding import PartitionSpec as P

DOC_DEV = 8
F32 = jnp.float32
BF16 = jnp.bfloat16
NT = (((1,), (1,)), ((), ()))
VMEM = pl.BlockSpec(memory_space=pltpu.VMEM)
HBM = pl.BlockSpec(memory_space=pltpu.HBM)
SMALL = pltpu.CompilerParams(vmem_limit_bytes=8 * 2**20)
PIECES = 2
STEPS = 32000.0
TAIL = 16


def swapped(block, axis, flip):
    return lax.ppermute(block, axis, [(i, i ^ flip) for i in range(lax.axis_size(axis))])


def encode(out, dx, dg):
    rank, chunk = dx.shape
    exponents = []
    for at, v in ((0, dx), (rank, dg)):
        top = jnp.maximum(jnp.max(jnp.abs(v), axis=0, keepdims=True), 1e-30)
        e = jnp.floor(jnp.log2(top)) + 1.0
        scaled = jnp.clip(jnp.round(v * (jnp.exp2(-e) * STEPS)), -32767.0, 32767.0)
        out[at : at + rank, :] = scaled.astype(jnp.int32).astype(jnp.int16)
        exponents.append(e.astype(jnp.int32))
    row = lax.broadcasted_iota(jnp.int32, (TAIL, chunk), 0)
    out[2 * rank :, :] = jnp.where(row == 0, exponents[0], jnp.where(row == 1, exponents[1], 0)).astype(jnp.int16)


def decode(part, rank):
    v = part[...].astype(jnp.int32).astype(F32)
    unit = jnp.exp2(v[2 * rank : 2 * rank + 2]) * (1.0 / STEPS)
    return v[:rank] * unit[0:1], v[rank : 2 * rank] * unit[1:2]


def project_kernel(flips, x_hbm, g_hbm, px_hbm, pg_hbm, *rest):
    outs, (xb, gb, px, pg, accx, accg, sems, wsems) = rest[: len(flips)], rest[len(flips) :]
    me = lax.axis_index("tensor")
    rank, chunk = px.shape[0], xb.shape[1]
    kx, kg = xb.shape[2], gb.shape[2]
    total = len(flips) * PIECES

    def copies(p):
        row = pl.multiple_of((me ^ flips[p // PIECES]) * chunk, chunk)
        i = p % PIECES
        return (
            pltpu.make_async_copy(x_hbm.at[pl.ds(row, chunk), pl.ds(i * kx, kx)], xb.at[p], sems.at[0, p]),
            pltpu.make_async_copy(g_hbm.at[pl.ds(row, chunk), pl.ds(i * kg, kg)], gb.at[p], sems.at[1, p]),
        )

    weights = (
        pltpu.make_async_copy(px_hbm, px, wsems.at[0]),
        pltpu.make_async_copy(pg_hbm, pg, wsems.at[1]),
    )
    for c in weights:
        c.start()
    ahead = min(2, total)
    for p in range(ahead):
        for c in copies(p):
            c.start()
    for c in weights:
        c.wait()
    for p in range(total):
        i, out = p % PIECES, outs[p // PIECES]
        for c in copies(p):
            c.wait()
        if p + ahead < total:
            for c in copies(p + ahead):
                c.start()

        @pl.when(me >= 0)
        def _():
            dx = lax.dot_general(xb[p], px[:, i * kx : (i + 1) * kx], NT, preferred_element_type=F32)
            dg = lax.dot_general(gb[p], pg[:, i * kg : (i + 1) * kg], NT, preferred_element_type=F32)
            if i > 0:
                dx, dg = dx + accx[...], dg + accg[...]
            if i < PIECES - 1:
                accx[...], accg[...] = dx, dg
            else:
                dx, dg = dx.T, dg.T
                if flips[p // PIECES]:
                    encode(out, dx, dg)
                else:
                    out[:rank, :], out[rank:, :] = dx, dg


def project(flips, inputs, grads, proj_in_t, proj_out_t, chunk):
    rank = proj_in_t.shape[0]
    total = len(flips) * PIECES
    kx, kg = inputs.shape[1] // PIECES, grads.shape[1] // PIECES
    return pl.pallas_call(
        functools.partial(project_kernel, flips),
        out_shape=[
            jax.ShapeDtypeStruct((2 * rank + TAIL, chunk), jnp.int16)
            if k
            else jax.ShapeDtypeStruct((2 * rank, chunk), F32)
            for k in flips
        ],
        in_specs=[HBM] * 4,
        out_specs=[VMEM] * len(flips),
        scratch_shapes=[
            pltpu.VMEM((total, chunk, kx), BF16),
            pltpu.VMEM((total, chunk, kg), BF16),
            pltpu.VMEM(proj_in_t.shape, BF16),
            pltpu.VMEM(proj_out_t.shape, BF16),
            pltpu.VMEM((chunk, rank), F32),
            pltpu.VMEM((chunk, rank), F32),
            pltpu.SemaphoreType.DMA((2, total)),
            pltpu.SemaphoreType.DMA((2,)),
        ],
        compiler_params=pltpu.CompilerParams(vmem_limit_bytes=int(53.5 * 2**20)),
        name="project",
    )(inputs, grads, proj_in_t, proj_out_t)


def outer_kernel(shares, ids, *refs):
    parts, outs, (prod,) = refs[:shares], refs[shares : 2 * shares], refs[2 * shares :]
    me = lax.axis_index("tensor")
    rank, chunk = parts[0].shape[0] // 2, parts[0].shape[1]
    x, g = parts[0][:rank], parts[0][rank:]
    for part in parts[1:]:
        more_x, more_g = decode(part, rank)
        x, g = x + more_x, g + more_g
    own = ids[:, pl.ds(pl.multiple_of(me * chunk, chunk), chunk)]
    mask = own == lax.broadcasted_iota(jnp.int32, (DOC_DEV, chunk), 0)
    rows = jnp.concatenate([jnp.where(mask, g[i : i + 1], 0.0) for i in range(rank)], axis=0)
    rows_hi = rows.astype(BF16)
    rows_lo = (rows - rows_hi.astype(F32)).astype(BF16)
    x_hi = x.astype(BF16)
    x_lo = (x - x_hi.astype(F32)).astype(BF16)
    dot = functools.partial(lax.dot_general, dimension_numbers=NT, preferred_element_type=F32)
    total = dot(rows_hi, x_hi) + (dot(rows_hi, x_lo) + dot(rows_lo, x_hi))
    prod[...] = total.reshape(rank, DOC_DEV, rank)
    share = rank // shares
    for k in range(shares):
        first = (me ^ k) * share
        outs[k][...] = jnp.concatenate([prod[first + r] for r in range(share)], axis=1)


def outer(parts, ids):
    shares = len(parts)
    rank = parts[0].shape[0] // 2
    return pl.pallas_call(
        functools.partial(outer_kernel, shares),
        out_shape=[jax.ShapeDtypeStruct((DOC_DEV, rank * rank // shares), F32)] * shares,
        in_specs=[VMEM] * (1 + shares),
        out_specs=[VMEM] * shares,
        scratch_shapes=[pltpu.VMEM((rank, DOC_DEV, rank), F32)],
        compiler_params=SMALL,
        name="outer",
    )(ids, *parts)


def train_kernel(ids, *refs):
    parts, out = refs[:-1], refs[-1]
    total = parts[0][...]
    for part in parts[1:]:
        total = total + part[...]
    hits = ids[...] == lax.broadcasted_iota(jnp.int32, (DOC_DEV, ids.shape[1]), 0)
    counts = jnp.sum(hits.astype(F32), axis=1, keepdims=True)
    train = total / counts
    half = train.shape[1] // 2
    out[...] = jnp.concatenate([train[:, :half], train[:, half:]], axis=0).astype(BF16)


def mean_gradients(parts, ids):
    width = parts[0].shape[1]
    return pl.pallas_call(
        train_kernel,
        out_shape=jax.ShapeDtypeStruct((2 * DOC_DEV, width // 2), BF16),
        in_specs=[VMEM] * (1 + len(parts)),
        out_specs=VMEM,
        compiler_params=SMALL,
        name="train",
    )(ids, *parts)


def score_kernel(shares, chips, *refs):
    blocks, trains, outs, (held,) = refs[:chips], refs[chips : chips + 2], refs[chips + 2 : -1], refs[-1:]
    me = lax.axis_index("tensor")
    rows = []
    for train in trains:
        t = train[...].astype(F32)
        rows.append(jnp.concatenate([t[:DOC_DEV], t[DOC_DEV:]], axis=1))
    docs = jnp.concatenate(rows, axis=0).astype(BF16)
    count = docs.shape[0]
    width = blocks[0].shape[0] // shares
    for m, queries in enumerate(blocks):
        scores = lax.dot_general(docs, queries[...], NT, preferred_element_type=F32)
        for j in range(shares):
            held[j, m * count : (m + 1) * count, :] = scores[:, j * width : (j + 1) * width]
    for k in range(shares):
        outs[k][...] = held[me ^ k]


def score(trains, blocks, shares):
    shape = (2 * DOC_DEV * len(blocks), blocks[0].shape[0] // shares)
    return pl.pallas_call(
        functools.partial(score_kernel, shares, len(blocks)),
        out_shape=[jax.ShapeDtypeStruct(shape, F32)] * shares,
        in_specs=[VMEM] * (len(blocks) + len(trains)),
        out_specs=[VMEM] * shares,
        scratch_shapes=[pltpu.VMEM((shares, *shape), F32)],
        compiler_params=SMALL,
        name="score",
    )(*blocks, *trains)


def add_kernel(shares, *refs):
    parts, outs = refs[:shares], refs[shares:]
    total = parts[0][...]
    for part in parts[1:]:
        total = total + part[...]
    both = total.reshape(-1, 2, DOC_DEV, total.shape[1])
    for core, out in enumerate(outs):
        out[...] = both[:, core]


def add(parts):
    rows, width = parts[0].shape
    return pl.pallas_call(
        functools.partial(add_kernel, len(parts)),
        out_shape=[jax.ShapeDtypeStruct((rows // (2 * DOC_DEV), DOC_DEV, width), F32)] * 2,
        in_specs=[VMEM] * len(parts),
        out_specs=[VMEM] * 2,
        compiler_params=SMALL,
        name="add",
    )(*parts)


def place_kernel(near, far, out):
    me = lax.axis_index("docs")
    for m in range(near.shape[0]):
        out[:, pl.ds(me ^ (2 * m), 1), :] = near[m][:, None, :]
        out[:, pl.ds(me ^ (2 * m + 1), 1), :] = far[m][:, None, :]


def place(near, far):
    chips, docs, width = near.shape
    return pl.pallas_call(
        place_kernel,
        out_shape=jax.ShapeDtypeStruct((docs, 2 * chips, width), F32),
        in_specs=[VMEM] * 2,
        out_specs=VMEM,
        compiler_params=SMALL,
        name="place",
    )(near, far)


def groups_of(shares):
    flips = list(range(shares - 1, -1, -1))
    return [flips[:-1], flips[-1:]]


def per_device(inputs, grads, proj_in, proj_out, queries, ids):
    shares, ndev = lax.axis_size("tensor"), lax.axis_size("docs")
    chips = ndev // 2
    chunk = inputs.shape[0] // shares
    blocks = [queries] + [swapped(queries, "docs", 2 * m) for m in range(1, chips)]
    flips = list(range(shares - 1, 0, -1))
    parts = {}
    for group in groups_of(shares):
        made = project(group, inputs, grads, proj_in.T, proj_out.T, chunk)
        for k, part in zip(group, made):
            parts[k] = swapped(part, "tensor", k) if k else part
    sums = outer([parts[k] for k in range(shares)], ids)
    arrived = [swapped(sums[k], "tensor", k) for k in flips]
    train = mean_gradients([sums[0]] + arrived, ids)
    scores = score([train, swapped(train, "docs", 1)], blocks, shares)
    arrived = [swapped(scores[k], "tensor", k) for k in flips]
    mine, sibling = add([scores[0]] + arrived)
    return place(mine, swapped(sibling, "docs", 1))


def solution(mesh):
    in_specs = (
        P(("group", "docs"), "tensor"),
        P(("group", "docs"), "tensor"),
        P("tensor", None),
        P("tensor", None),
        P(("group", "docs"), "tensor"),
        P(("group", "docs"), None),
    )
    out_specs = P(("group", "docs"), None, "tensor")
    return jax.shard_map(
        per_device, mesh=mesh, in_specs=in_specs, out_specs=out_specs, check_vma=False
    )
```

```python
import functools

import jax
import jax.numpy as jnp
from jax import lax
from jax.experimental import pallas as pl
from jax.experimental.pallas import tpu as pltpu
from jax.sharding import PartitionSpec as P

DOC_DEV = 8
F32 = jnp.float32
BF16 = jnp.bfloat16
NT = (((1,), (1,)), ((), ()))
VMEM = pl.BlockSpec(memory_space=pltpu.VMEM)
SMALL = pltpu.CompilerParams(vmem_limit_bytes=8 * 2**20)
STEPS = 32000.0
LANES = 128


def swapped(block, axis, flip):
    return lax.ppermute(block, axis, [(i, i ^ flip) for i in range(lax.axis_size(axis))])


def crossed(block, core, flip):
    shares, ndev = lax.axis_size("tensor"), lax.axis_size("docs")
    pairs = [(d * shares + s, (d ^ core) * shares + (s ^ flip)) for d in range(ndev) for s in range(shares)]
    return lax.ppermute(block, ("docs", "tensor"), pairs)


def coded(v):
    top = jnp.maximum(jnp.max(jnp.abs(v), axis=0, keepdims=True), 1e-30)
    e = jnp.floor(jnp.log2(top)) + 1.0
    steps = jnp.clip(jnp.round(v * (jnp.exp2(-e) * STEPS)), -32767.0, 32767.0)
    return steps.astype(jnp.int32), e.astype(jnp.int32)


def decoded(steps, e):
    return steps.astype(jnp.int32).astype(F32) * (jnp.exp2(e.astype(F32)) * (1.0 / STEPS))


def folded(e):
    return jnp.concatenate([e[:, a : a + LANES] for a in range(0, e.shape[1], LANES)], axis=0)


def unfolded(e):
    return jnp.concatenate([e[a : a + 1] for a in range(e.shape[0])], axis=1)


def projected(rows, weights):
    step = 256
    parts = [
        lax.dot_general(rows[a : a + step, :], weights[...], NT, preferred_element_type=F32).T
        for a in range(0, rows.shape[0], step)
    ]
    return jnp.concatenate(parts, axis=1)


def write_message(sent, v):
    steps, e = coded(v)
    tokens = v.shape[1]
    sent[:, :tokens] = steps.astype(jnp.int16)
    tail = folded(e)
    blank = jnp.zeros((v.shape[0] - tail.shape[0], LANES), jnp.int32)
    sent[:, tokens:] = jnp.concatenate([tail, blank], axis=0).astype(jnp.int16)


def read_message(sent):
    tokens = sent.shape[1] - LANES
    tail = sent[:, tokens:].astype(jnp.int32)
    return decoded(sent[:, :tokens], unfolded(tail[: tokens // LANES]))


def inputs_kernel(x, px, own, sent):
    v = projected(x, px)
    own[...] = v
    write_message(sent, v)


def fold_in_kernel(own, arrived, total, sent):
    v = own[...] + read_message(arrived)
    total[...] = v
    write_message(sent, v)


def fold_in(own, arrived):
    return pl.pallas_call(
        fold_in_kernel,
        out_shape=[jax.ShapeDtypeStruct(own.shape, F32), jax.ShapeDtypeStruct(arrived.shape, jnp.int16)],
        in_specs=[VMEM] * 2,
        out_specs=[VMEM] * 2,
        compiler_params=SMALL,
        name="fold_in",
    )(own, arrived)


def project_inputs(inputs, proj_t):
    rank, tokens = proj_t.shape[0], inputs.shape[0]
    return pl.pallas_call(
        inputs_kernel,
        out_shape=[
            jax.ShapeDtypeStruct((rank, tokens), F32),
            jax.ShapeDtypeStruct((rank, tokens + LANES), jnp.int16),
        ],
        in_specs=[VMEM] * 2,
        out_specs=[VMEM] * 2,
        compiler_params=SMALL,
        cost_estimate=pl.CostEstimate(flops=20_000_000_000, bytes_accessed=4_000_000, transcendentals=0),
        name="inputs",
    )(inputs, proj_t)


def grads_kernel(shares, g, pg, own, *rest):
    outs, held = rest[:-1], rest[-1]
    me = lax.axis_index("tensor")
    v = projected(g, pg)
    rank, tokens = v.shape
    rows = rank // shares
    steps, e = coded(v)
    tail = folded(e)
    if rows > tail.shape[0]:
        tail = jnp.concatenate([tail, jnp.zeros((rows - tail.shape[0], LANES), jnp.int32)], axis=0)
    tail = tail.astype(jnp.int16)
    held[...] = v.reshape(shares, rows, tokens)
    own[...] = held[me]
    held[...] = steps.astype(F32).reshape(shares, rows, tokens)
    for k, out in enumerate(outs):
        out[:, :tokens] = held[me ^ (len(outs) - k)].astype(jnp.int32).astype(jnp.int16)
        out[:, tokens:] = tail


def project_grads(grads, proj_t, shares):
    rank, tokens = proj_t.shape[0], grads.shape[0]
    rows = rank // shares
    return pl.pallas_call(
        functools.partial(grads_kernel, shares),
        out_shape=[jax.ShapeDtypeStruct((rows, tokens), F32)]
        + [jax.ShapeDtypeStruct((rows, tokens + LANES), jnp.int16)] * (shares - 1),
        in_specs=[VMEM] * 2,
        out_specs=[VMEM] * shares,
        scratch_shapes=[pltpu.VMEM((shares, rows, tokens), F32)],
        compiler_params=SMALL,
        name="grads",
    )(grads, proj_t)


def train_kernel(ids, x_own, x_sent, g_own, *refs):
    g_sent, out = refs[:-1], refs[-1]
    x, g = x_own[...] + read_message(x_sent), g_own[...]
    for sent in g_sent:
        g = g + read_message(sent)
    rows, tokens = g.shape
    mask = ids[...] == lax.broadcasted_iota(jnp.int32, (DOC_DEV, tokens), 0)
    counts = jnp.sum(mask.astype(F32), axis=1, keepdims=True)
    picked = jnp.concatenate([jnp.where(mask, g[i : i + 1], 0.0) for i in range(rows)], axis=0)
    picked_hi = picked.astype(BF16)
    picked_lo = (picked - picked_hi.astype(F32)).astype(BF16)
    x_hi = x.astype(BF16)
    x_lo = (x - x_hi.astype(F32)).astype(BF16)
    dot = functools.partial(lax.dot_general, dimension_numbers=NT, preferred_element_type=F32)
    total = dot(picked_hi, x_hi) + (dot(picked_hi, x_lo) + dot(picked_lo, x_hi))
    train = jnp.concatenate([total[i * DOC_DEV : (i + 1) * DOC_DEV] for i in range(rows)], axis=1) / counts
    half = train.shape[1] // 2
    out[...] = jnp.concatenate([train[:, :half], train[:, half:]], axis=0).astype(BF16)


def mean_gradients(ids, x_own, x_sent, g_own, g_sent):
    width = g_own.shape[0] * x_own.shape[0]
    return pl.pallas_call(
        train_kernel,
        out_shape=jax.ShapeDtypeStruct((2 * DOC_DEV, width // 2), BF16),
        in_specs=[VMEM] * (4 + len(g_sent)),
        out_specs=VMEM,
        compiler_params=SMALL,
        name="train",
    )(ids, x_own, x_sent, g_own, *g_sent)


def scores_of(trains, queries):
    rows = []
    for train in trains:
        t = train[...].astype(F32)
        rows.append(jnp.concatenate([t[:DOC_DEV], t[DOC_DEV:]], axis=1))
    docs = jnp.concatenate(rows, axis=0).astype(BF16)
    return lax.dot_general(docs, queries[...], NT, preferred_element_type=F32)


def near_kernel(mine, sibling, queries, out):
    out[...] = scores_of((mine, sibling), queries)


def score_kernel(shares, mine, sibling, near, *refs):
    blocks, outs, held = refs[: -shares - 1], refs[-shares - 1 : -1], refs[-1]
    me = lax.axis_index("tensor")
    count, width = near.shape[0], near.shape[1] // shares
    for m in range(len(blocks) + 1):
        scores = scores_of((mine, sibling), blocks[m - 1]) if m else near[...]
        for j in range(shares):
            held[j, m * count : (m + 1) * count, :] = scores[:, j * width : (j + 1) * width]
    for k in range(shares):
        outs[k][...] = held[me ^ k]


def score(mine, sibling, blocks, shares):
    rows, width = 2 * DOC_DEV, blocks[0].shape[0]
    near = pl.pallas_call(
        near_kernel,
        out_shape=jax.ShapeDtypeStruct((rows, width), F32),
        in_specs=[VMEM] * 3,
        out_specs=VMEM,
        compiler_params=SMALL,
        name="near",
    )(mine, sibling, blocks[0])
    shape = (rows * len(blocks), width // shares)
    return pl.pallas_call(
        functools.partial(score_kernel, shares),
        out_shape=[jax.ShapeDtypeStruct(shape, F32)] * shares,
        in_specs=[VMEM] * (2 + len(blocks)),
        out_specs=[VMEM] * shares,
        scratch_shapes=[pltpu.VMEM((shares, *shape), F32)],
        compiler_params=SMALL,
        name="score",
    )(mine, sibling, near, *blocks[1:])


def add_kernel(shares, *refs):
    parts, outs = refs[:shares], refs[shares:]
    total = parts[0][...]
    for part in parts[1:]:
        total = total + part[...]
    both = total.reshape(-1, 2, DOC_DEV, total.shape[1])
    for core, out in enumerate(outs):
        out[...] = both[:, 1 - core]


def add(parts):
    rows, width = parts[0].shape
    return pl.pallas_call(
        functools.partial(add_kernel, len(parts)),
        out_shape=[jax.ShapeDtypeStruct((rows // (2 * DOC_DEV), DOC_DEV, width), F32)] * 2,
        in_specs=[VMEM] * len(parts),
        out_specs=[VMEM] * 2,
        compiler_params=SMALL,
        name="add",
    )(*parts)


def place_kernel(near, far, out):
    me = lax.axis_index("docs")
    for m in range(near.shape[0]):
        out[:, pl.ds(me ^ (2 * m + 1), 1), :] = near[m][:, None, :]
        out[:, pl.ds(me ^ (2 * m), 1), :] = far[m][:, None, :]


def place(near, far):
    chips, docs, width = near.shape
    return pl.pallas_call(
        place_kernel,
        out_shape=jax.ShapeDtypeStruct((docs, 2 * chips, width), F32),
        in_specs=[VMEM] * 2,
        out_specs=VMEM,
        compiler_params=SMALL,
        name="place",
    )(near, far)


def per_device(inputs, grads, proj_in, proj_out, queries, ids):
    shares, ndev = lax.axis_size("tensor"), lax.axis_size("docs")
    blocks = [queries] + [swapped(queries, "docs", 2 * m) for m in range(1, ndev // 2)]
    flips = list(range(shares - 1, 0, -1))
    x, x_sent = project_inputs(inputs, proj_in.T)
    flip = shares // 2
    x_sent = swapped(x_sent, "tensor", flip)
    g_own, *g_coded = project_grads(grads, proj_out.T, shares)
    x_sent, g_own = lax.optimization_barrier((x_sent, g_own))
    while flip > 1:
        flip //= 2
        x, x_sent = fold_in(x, x_sent)
        x_sent = swapped(x_sent, "tensor", flip)
    g_sent = [swapped(g, "tensor", k) for k, g in zip(flips, g_coded)]
    train = mean_gradients(ids, x, x_sent, g_own, g_sent)
    scores = score(train, swapped(train, "docs", 1), blocks, shares)
    mine, sibling = add([crossed(scores[k], 1, k) for k in flips + [0]])
    return place(mine, swapped(sibling, "docs", 1))


def solution(mesh):
    in_specs = (
        P(("group", "docs"), "tensor"),
        P(("group", "docs"), "tensor"),
        P("tensor", None),
        P("tensor", None),
        P(("group", "docs"), "tensor"),
        P(("group", "docs"), None),
    )
    out_specs = P(("group", "docs"), None, "tensor")
    return jax.shard_map(
        per_device, mesh=mesh, in_specs=in_specs, out_specs=out_specs, check_vma=False
    )
```

```python
import functools

import jax
import jax.numpy as jnp
from jax import lax
from jax.experimental import pallas as pl
from jax.experimental.pallas import tpu as pltpu
from jax.sharding import PartitionSpec as P

DOC_DEV = 8
F32 = jnp.float32
BF16 = jnp.bfloat16
NT = (((1,), (1,)), ((), ()))
VMEM = pl.BlockSpec(memory_space=pltpu.VMEM)
ANY = pl.BlockSpec(memory_space=pl.ANY)
STREAM = pltpu.CompilerParams(vmem_limit_bytes=int(53.5 * 2**20))
SMALL = pltpu.CompilerParams(vmem_limit_bytes=8 * 2**20)
STEPS = 32000.0
LANES = 128
ROW_STEPS = 4
X_PIECES, X_AHEAD = 1, 4
G_PIECES, G_AHEAD = 1, 2


def swapped(block, axis, flip):
    return lax.ppermute(block, axis, [(i, i ^ flip) for i in range(lax.axis_size(axis))])


def crossed(block, core, flip):
    shares, ndev = lax.axis_size("tensor"), lax.axis_size("docs")
    pairs = [(d * shares + s, (d ^ core) * shares + (s ^ flip)) for d in range(ndev) for s in range(shares)]
    return lax.ppermute(block, ("docs", "tensor"), pairs)


def coded(v):
    top = jnp.maximum(jnp.max(jnp.abs(v), axis=0, keepdims=True), 1e-30)
    e = jnp.floor(jnp.log2(top)) + 1.0
    steps = jnp.clip(jnp.round(v * (jnp.exp2(-e) * STEPS)), -32767.0, 32767.0)
    return steps.astype(jnp.int32), e.astype(jnp.int32)


def decoded(steps, e):
    return steps.astype(jnp.int32).astype(F32) * (jnp.exp2(e.astype(F32)) * (1.0 / STEPS))


def folded(e):
    return jnp.concatenate([e[:, a : a + LANES] for a in range(0, e.shape[1], LANES)], axis=0)


def unfolded(e):
    return jnp.concatenate([e[a : a + 1] for a in range(e.shape[0])], axis=1)


def write_message(sent, v):
    steps, e = coded(v)
    tokens = v.shape[1]
    sent[:, :tokens] = steps.astype(jnp.int16)
    tail = folded(e)
    blank = jnp.zeros((v.shape[0] - tail.shape[0], LANES), jnp.int32)
    sent[:, tokens:] = jnp.concatenate([tail, blank], axis=0).astype(jnp.int16)


def read_message(sent):
    tokens = sent.shape[1] - LANES
    tail = sent[:, tokens:].astype(jnp.int32)
    return decoded(sent[:, :tokens], unfolded(tail[: tokens // LANES]))


def stream_copies(hbm, buffer, sems, pieces):
    rows, columns = buffer.shape[0] // ROW_STEPS, buffer.shape[1] // pieces
    return [
        pltpu.make_async_copy(
            hbm.at[pl.ds(a * rows, rows), pl.ds(c * columns, columns)],
            buffer.at[pl.ds(a * rows, rows), pl.ds(c * columns, columns)],
            sems.at[a * pieces + c],
        )
        for a in range(ROW_STEPS)
        for c in range(pieces)
    ]


def streamed(hbm, weights_hbm, buffer, weights, acc, out, sems, pieces, ahead):
    me = lax.axis_index("tensor")
    rows, columns = buffer.shape[0] // ROW_STEPS, buffer.shape[1] // pieces
    copies = stream_copies(hbm, buffer, sems, pieces)
    first = pltpu.make_async_copy(weights_hbm, weights, sems.at[len(copies)])
    first.start()
    for copy in copies[:ahead]:
        copy.start()
    first.wait()
    for t, copy in enumerate(copies):
        copy.wait()
        if t + ahead < len(copies):
            copies[t + ahead].start()
        a, c = t // pieces, t % pieces

        @pl.when(me >= 0)
        def _():
            d = lax.dot_general(
                buffer[a * rows : (a + 1) * rows, c * columns : (c + 1) * columns],
                weights[:, c * columns : (c + 1) * columns],
                NT,
                preferred_element_type=F32,
            )
            if c > 0:
                d = d + acc[...]
            if c < pieces - 1:
                acc[...] = d
            else:
                out[:, a * rows : (a + 1) * rows] = d.T


def stream_scratch(rows, proj_t, pieces):
    return [
        pltpu.VMEM((rows, proj_t.shape[1]), BF16),
        pltpu.VMEM(proj_t.shape, BF16),
        pltpu.VMEM((rows // ROW_STEPS, proj_t.shape[0]), F32),
        pltpu.SemaphoreType.DMA((ROW_STEPS * pieces + 1,)),
    ]


def inputs_kernel(x_hbm, px_hbm, own, sent, x, px, acc, sems):
    streamed(x_hbm, px_hbm, x, px, acc, own, sems, X_PIECES, X_AHEAD)
    write_message(sent, own[...])


def fold_in_kernel(own, arrived, total, sent):
    v = own[...] + read_message(arrived)
    total[...] = v
    write_message(sent, v)


def fold_in(own, arrived):
    return pl.pallas_call(
        fold_in_kernel,
        out_shape=[jax.ShapeDtypeStruct(own.shape, F32), jax.ShapeDtypeStruct(arrived.shape, jnp.int16)],
        in_specs=[VMEM] * 2,
        out_specs=[VMEM] * 2,
        compiler_params=SMALL,
        name="fold_in",
    )(own, arrived)


def project_inputs(inputs, proj_t):
    rank, tokens = proj_t.shape[0], inputs.shape[0]
    return pl.pallas_call(
        inputs_kernel,
        out_shape=[
            jax.ShapeDtypeStruct((rank, tokens), F32),
            jax.ShapeDtypeStruct((rank, tokens + LANES), jnp.int16),
        ],
        in_specs=[ANY] * 2,
        out_specs=[VMEM] * 2,
        scratch_shapes=stream_scratch(tokens, proj_t, X_PIECES),
        compiler_params=STREAM,
        name="inputs",
    )(inputs, proj_t)


def grads_kernel(shares, g_hbm, pg_hbm, own, *rest):
    outs, (held, full, g, pg, acc, sems) = rest[: shares - 1], rest[shares - 1 :]
    streamed(g_hbm, pg_hbm, g, pg, acc, full, sems, G_PIECES, G_AHEAD)
    me = lax.axis_index("tensor")
    v = full[...]
    rank, tokens = v.shape
    rows = rank // shares
    steps, e = coded(v)
    tail = folded(e)
    if rows > tail.shape[0]:
        tail = jnp.concatenate([tail, jnp.zeros((rows - tail.shape[0], LANES), jnp.int32)], axis=0)
    tail = tail.astype(jnp.int16)
    held[...] = v.reshape(shares, rows, tokens)
    own[...] = held[me]
    held[...] = steps.astype(F32).reshape(shares, rows, tokens)
    for k, out in enumerate(outs):
        out[:, :tokens] = held[me ^ (len(outs) - k)].astype(jnp.int32).astype(jnp.int16)
        out[:, tokens:] = tail


def project_grads(grads, proj_t, shares):
    rank, tokens = proj_t.shape[0], grads.shape[0]
    rows = rank // shares
    return pl.pallas_call(
        functools.partial(grads_kernel, shares),
        out_shape=[jax.ShapeDtypeStruct((rows, tokens), F32)]
        + [jax.ShapeDtypeStruct((rows, tokens + LANES), jnp.int16)] * (shares - 1),
        in_specs=[ANY] * 2,
        out_specs=[VMEM] * shares,
        scratch_shapes=[pltpu.VMEM((shares, rows, tokens), F32), pltpu.VMEM((rank, tokens), F32)]
        + stream_scratch(tokens, proj_t, G_PIECES),
        compiler_params=STREAM,
        name="grads",
    )(grads, proj_t)


def train_kernel(ids, x_own, x_sent, g_own, *refs):
    g_sent, out = refs[:-1], refs[-1]
    x, g = x_own[...] + read_message(x_sent), g_own[...]
    for sent in g_sent:
        g = g + read_message(sent)
    rows, tokens = g.shape
    mask = ids[...] == lax.broadcasted_iota(jnp.int32, (DOC_DEV, tokens), 0)
    counts = jnp.sum(mask.astype(F32), axis=1, keepdims=True)
    picked = jnp.concatenate([jnp.where(mask, g[i : i + 1], 0.0) for i in range(rows)], axis=0)
    picked_hi = picked.astype(BF16)
    picked_lo = (picked - picked_hi.astype(F32)).astype(BF16)
    x_hi = x.astype(BF16)
    x_lo = (x - x_hi.astype(F32)).astype(BF16)
    dot = functools.partial(lax.dot_general, dimension_numbers=NT, preferred_element_type=F32)
    total = dot(picked_hi, x_hi) + (dot(picked_hi, x_lo) + dot(picked_lo, x_hi))
    train = jnp.concatenate([total[i * DOC_DEV : (i + 1) * DOC_DEV] for i in range(rows)], axis=1) / counts
    half = train.shape[1] // 2
    out[...] = jnp.concatenate([train[:, :half], train[:, half:]], axis=0).astype(BF16)


def mean_gradients(ids, x_own, x_sent, g_own, g_sent):
    width = g_own.shape[0] * x_own.shape[0]
    return pl.pallas_call(
        train_kernel,
        out_shape=jax.ShapeDtypeStruct((2 * DOC_DEV, width // 2), BF16),
        in_specs=[VMEM] * (4 + len(g_sent)),
        out_specs=VMEM,
        compiler_params=SMALL,
        name="train",
    )(ids, x_own, x_sent, g_own, *g_sent)


def scores_of(trains, queries):
    rows = []
    for train in trains:
        t = train[...].astype(F32)
        rows.append(jnp.concatenate([t[:DOC_DEV], t[DOC_DEV:]], axis=1))
    docs = jnp.concatenate(rows, axis=0).astype(BF16)
    return lax.dot_general(docs, queries[...], NT, preferred_element_type=F32)


def near_kernel(mine, sibling, queries, out):
    out[...] = scores_of((mine, sibling), queries)


def score_kernel(shares, mine, sibling, near, *refs):
    blocks, outs, held = refs[: -shares - 1], refs[-shares - 1 : -1], refs[-1]
    me = lax.axis_index("tensor")
    count, width = near.shape[0], near.shape[1] // shares
    for m in range(len(blocks) + 1):
        scores = scores_of((mine, sibling), blocks[m - 1]) if m else near[...]
        for j in range(shares):
            held[j, m * count : (m + 1) * count, :] = scores[:, j * width : (j + 1) * width]
    for k in range(shares):
        outs[k][...] = held[me ^ k]


def score(mine, sibling, blocks, shares):
    rows, width = 2 * DOC_DEV, blocks[0].shape[0]
    near = pl.pallas_call(
        near_kernel,
        out_shape=jax.ShapeDtypeStruct((rows, width), F32),
        in_specs=[VMEM] * 3,
        out_specs=VMEM,
        compiler_params=SMALL,
        name="near",
    )(mine, sibling, blocks[0])
    shape = (rows * len(blocks), width // shares)
    return pl.pallas_call(
        functools.partial(score_kernel, shares),
        out_shape=[jax.ShapeDtypeStruct(shape, F32)] * shares,
        in_specs=[VMEM] * (2 + len(blocks)),
        out_specs=[VMEM] * shares,
        scratch_shapes=[pltpu.VMEM((shares, *shape), F32)],
        compiler_params=SMALL,
        name="score",
    )(mine, sibling, near, *blocks[1:])


def add_kernel(shares, *refs):
    parts, outs = refs[:shares], refs[shares:]
    total = parts[0][...]
    for part in parts[1:]:
        total = total + part[...]
    both = total.reshape(-1, 2, DOC_DEV, total.shape[1])
    for core, out in enumerate(outs):
        out[...] = both[:, 1 - core]


def add(parts):
    rows, width = parts[0].shape
    return pl.pallas_call(
        functools.partial(add_kernel, len(parts)),
        out_shape=[jax.ShapeDtypeStruct((rows // (2 * DOC_DEV), DOC_DEV, width), F32)] * 2,
        in_specs=[VMEM] * len(parts),
        out_specs=[VMEM] * 2,
        compiler_params=SMALL,
        name="add",
    )(*parts)


def place_kernel(near, far, out):
    me = lax.axis_index("docs")
    for m in range(near.shape[0]):
        out[:, pl.ds(me ^ (2 * m + 1), 1), :] = near[m][:, None, :]
        out[:, pl.ds(me ^ (2 * m), 1), :] = far[m][:, None, :]


def place(near, far):
    chips, docs, width = near.shape
    return pl.pallas_call(
        place_kernel,
        out_shape=jax.ShapeDtypeStruct((docs, 2 * chips, width), F32),
        in_specs=[VMEM] * 2,
        out_specs=VMEM,
        compiler_params=SMALL,
        name="place",
    )(near, far)


def per_device(inputs, grads, proj_in, proj_out, queries, ids):
    shares, ndev = lax.axis_size("tensor"), lax.axis_size("docs")
    blocks = [queries] + [swapped(queries, "docs", 2 * m) for m in range(1, ndev // 2)]
    flips = list(range(shares - 1, 0, -1))
    x, x_sent = project_inputs(inputs, proj_in.T)
    flip = shares // 2
    x_sent = swapped(x_sent, "tensor", flip)
    g_own, *g_coded = project_grads(grads, proj_out.T, shares)
    x_sent, g_own = lax.optimization_barrier((x_sent, g_own))
    while flip > 1:
        flip //= 2
        x, x_sent = fold_in(x, x_sent)
        x_sent = swapped(x_sent, "tensor", flip)
    g_sent = [swapped(g, "tensor", k) for k, g in zip(flips, g_coded)]
    train = mean_gradients(ids, x, x_sent, g_own, g_sent)
    scores = score(train, swapped(train, "docs", 1), blocks, shares)
    mine, sibling = add([crossed(scores[k], 1, k) for k in flips + [0]])
    return place(mine, swapped(sibling, "docs", 1))


def solution(mesh):
    in_specs = (
        P(("group", "docs"), "tensor"),
        P(("group", "docs"), "tensor"),
        P("tensor", None),
        P("tensor", None),
        P(("group", "docs"), "tensor"),
        P(("group", "docs"), None),
    )
    out_specs = P(("group", "docs"), None, "tensor")
    return jax.shard_map(
        per_device, mesh=mesh, in_specs=in_specs, out_specs=out_specs, check_vma=False
    )
```

```python
import functools

import jax
import jax.numpy as jnp
from jax import lax
from jax.experimental import pallas as pl
from jax.experimental.pallas import tpu as pltpu
from jax.sharding import PartitionSpec as P

DOC_DEV = 8
F32 = jnp.float32
BF16 = jnp.bfloat16
NT = (((1,), (1,)), ((), ()))
VMEM = pl.BlockSpec(memory_space=pltpu.VMEM)
ANY = pl.BlockSpec(memory_space=pl.ANY)
STREAM = pltpu.CompilerParams(vmem_limit_bytes=int(53.5 * 2**20))
SMALL = pltpu.CompilerParams(vmem_limit_bytes=8 * 2**20)
STEPS = 32000.0
LANES = 128
ROW_STEPS = 4
X_PIECES, X_AHEAD = 1, 4
G_PIECES, G_AHEAD = 1, 2


def swapped(block, axis, flip):
    return lax.ppermute(block, axis, [(i, i ^ flip) for i in range(lax.axis_size(axis))])


def crossed(block, core, flip):
    shares, ndev = lax.axis_size("tensor"), lax.axis_size("docs")
    pairs = [(d * shares + s, (d ^ core) * shares + (s ^ flip)) for d in range(ndev) for s in range(shares)]
    return lax.ppermute(block, ("docs", "tensor"), pairs)


def coded(v):
    top = jnp.maximum(jnp.max(jnp.abs(v), axis=0, keepdims=True), 1e-30)
    e = jnp.floor(jnp.log2(top)) + 1.0
    steps = jnp.clip(jnp.round(v * (jnp.exp2(-e) * STEPS)), -32767.0, 32767.0)
    return steps.astype(jnp.int32), e.astype(jnp.int32)


def decoded(steps, e):
    return steps.astype(jnp.int32).astype(F32) * (jnp.exp2(e.astype(F32)) * (1.0 / STEPS))


def folded(e):
    return jnp.concatenate([e[:, a : a + LANES] for a in range(0, e.shape[1], LANES)], axis=0)


def unfolded(e):
    return jnp.concatenate([e[a : a + 1] for a in range(e.shape[0])], axis=1)


def write_message(sent, v):
    steps, e = coded(v)
    rows, tokens = v.shape
    tail = folded(e)
    if rows > tail.shape[0]:
        tail = jnp.concatenate([tail, jnp.zeros((rows - tail.shape[0], LANES), jnp.int32)], axis=0)
    sent[:rows, :tokens] = steps.astype(jnp.int16)
    sent[:rows, tokens:] = tail.astype(jnp.int16)


def read_message(sent, first, rows):
    tokens = sent.shape[1] - LANES
    tail = sent[first : first + rows, tokens:].astype(jnp.int32)
    return decoded(sent[first : first + rows, :tokens], unfolded(tail[: tokens // LANES]))


def stream_copies(hbm, buffer, sems, pieces):
    rows, columns = buffer.shape[0] // ROW_STEPS, buffer.shape[1] // pieces
    return [
        pltpu.make_async_copy(
            hbm.at[pl.ds(a * rows, rows), pl.ds(c * columns, columns)],
            buffer.at[pl.ds(a * rows, rows), pl.ds(c * columns, columns)],
            sems.at[a * pieces + c],
        )
        for a in range(ROW_STEPS)
        for c in range(pieces)
    ]


def streamed(hbm, weights_hbm, buffer, weights, acc, out, sems, pieces, ahead, between=None):
    me = lax.axis_index("tensor")
    rows, columns = buffer.shape[0] // ROW_STEPS, buffer.shape[1] // pieces
    copies = stream_copies(hbm, buffer, sems, pieces)
    first = pltpu.make_async_copy(weights_hbm, weights, sems.at[len(copies)])
    first.start()
    for copy in copies[:ahead]:
        copy.start()
    if between:
        between(-1)
    first.wait()
    for t, copy in enumerate(copies):
        copy.wait()
        if t + ahead < len(copies):
            copies[t + ahead].start()
        if between:
            between(t)
        a, c = t // pieces, t % pieces

        @pl.when(me >= 0)
        def _():
            d = lax.dot_general(
                buffer[a * rows : (a + 1) * rows, c * columns : (c + 1) * columns],
                weights[:, c * columns : (c + 1) * columns],
                NT,
                preferred_element_type=F32,
            )
            if c > 0:
                d = d + acc[...]
            if c < pieces - 1:
                acc[...] = d
            else:
                out[:, a * rows : (a + 1) * rows] = d.T


def stream_scratch(rows, proj_t, pieces):
    return [
        pltpu.VMEM((rows, proj_t.shape[1]), BF16),
        pltpu.VMEM(proj_t.shape, BF16),
        pltpu.VMEM((rows // ROW_STEPS, proj_t.shape[0]), F32),
        pltpu.SemaphoreType.DMA((ROW_STEPS * pieces + 1,)),
    ]


def inputs_kernel(flips, x_hbm, px_hbm, queries, own, sent, early, late, x, px, acc, sems, staged, cuts):
    me = lax.axis_index("tensor")
    width = late.shape[0]
    staging = pltpu.make_async_copy(queries, staged, cuts.at[len(flips) + 1])
    pieces = [
        pltpu.make_async_copy(
            staged.at[pl.ds(pl.multiple_of((me ^ k) * width, width), width)],
            early.at[pl.ds(i * width, width)] if k else late,
            cuts.at[i],
        )
        for i, k in enumerate(flips + [0])
    ]

    def hand_on(step):
        if step < 0:
            staging.start()
        if step == 2:
            staging.wait()
            for piece in pieces:
                piece.start()

    streamed(x_hbm, px_hbm, x, px, acc, own, sems, X_PIECES, X_AHEAD, hand_on)
    write_message(sent, own[...])
    for piece in pieces:
        piece.wait()


def fold_in_kernel(own, arrived, total, sent):
    v = own[...] + read_message(arrived, 0, own.shape[0])
    total[...] = v
    write_message(sent, v)


def fold_in(own, arrived):
    return pl.pallas_call(
        fold_in_kernel,
        out_shape=[jax.ShapeDtypeStruct(own.shape, F32), jax.ShapeDtypeStruct(arrived.shape, jnp.int16)],
        in_specs=[VMEM] * 2,
        out_specs=[VMEM] * 2,
        compiler_params=SMALL,
        cost_estimate=pl.CostEstimate(flops=20_000_000_000, bytes_accessed=0, transcendentals=0),
        name="fold_in",
    )(own, arrived)


def project_inputs(inputs, proj_t, queries, flips):
    rank, tokens = proj_t.shape[0], inputs.shape[0]
    rows, width = queries.shape[0] // (len(flips) + 1), queries.shape[1]
    return pl.pallas_call(
        functools.partial(inputs_kernel, flips),
        out_shape=[
            jax.ShapeDtypeStruct((rank, tokens), F32),
            jax.ShapeDtypeStruct((rank, tokens + LANES), jnp.int16),
            jax.ShapeDtypeStruct((rows * len(flips), width), BF16),
            jax.ShapeDtypeStruct((rows, width), BF16),
        ],
        in_specs=[ANY] * 3,
        out_specs=[VMEM] * 2 + [ANY] * 2,
        scratch_shapes=stream_scratch(tokens, proj_t, X_PIECES)
        + [pltpu.VMEM(queries.shape, BF16), pltpu.SemaphoreType.DMA((len(flips) + 2,))],
        compiler_params=STREAM,
        name="inputs",
    )(inputs, proj_t, queries)


def grads_kernel(shares, g_hbm, pg_hbm, own, *rest):
    outs, (held, full, g, pg, acc, sems) = rest[: shares - 1], rest[shares - 1 :]
    streamed(g_hbm, pg_hbm, g, pg, acc, full, sems, G_PIECES, G_AHEAD)
    me = lax.axis_index("tensor")
    v = full[...]
    rank, tokens = v.shape
    rows = rank // shares
    steps, e = coded(v)
    tail = folded(e)
    if rows > tail.shape[0]:
        tail = jnp.concatenate([tail, jnp.zeros((rows - tail.shape[0], LANES), jnp.int32)], axis=0)
    tail = tail.astype(jnp.int16)
    held[...] = v.reshape(shares, rows, tokens)
    own[...] = held[me]
    held[...] = steps.astype(F32).reshape(shares, rows, tokens)
    for k, out in enumerate(outs):
        out[:, :tokens] = held[me ^ (len(outs) - k)].astype(jnp.int32).astype(jnp.int16)
        out[:, tokens:] = tail


def project_grads(grads, proj_t, shares):
    rank, tokens = proj_t.shape[0], grads.shape[0]
    rows = rank // shares
    return pl.pallas_call(
        functools.partial(grads_kernel, shares),
        out_shape=[jax.ShapeDtypeStruct((rows, tokens), F32)]
        + [jax.ShapeDtypeStruct((rows, tokens + LANES), jnp.int16)] * (shares - 1),
        in_specs=[ANY] * 2,
        out_specs=[VMEM] * shares,
        scratch_shapes=[pltpu.VMEM((shares, rows, tokens), F32), pltpu.VMEM((rank, tokens), F32)]
        + stream_scratch(tokens, proj_t, G_PIECES),
        compiler_params=pltpu.CompilerParams(vmem_limit_bytes=int(53.5 * 2**20)),
        name="grads",
    )(grads, proj_t)


def train_kernel(ids, x_own, g_own, x_sent, *refs):
    g_sent, out = refs[:-1], refs[-1]
    rank, rows = x_own.shape[0], g_own.shape[0]
    x, g = x_own[...] + read_message(x_sent, 0, rank), g_own[...]
    for sent in g_sent:
        g = g + read_message(sent, 0, rows)
    tokens = g.shape[1]
    mask = ids[...] == lax.broadcasted_iota(jnp.int32, (DOC_DEV, tokens), 0)
    counts = jnp.sum(mask.astype(F32), axis=1, keepdims=True)
    picked = jnp.concatenate([jnp.where(mask, g[i : i + 1], 0.0) for i in range(rows)], axis=0)
    picked_hi = picked.astype(BF16)
    picked_lo = (picked - picked_hi.astype(F32)).astype(BF16)
    x_hi = x.astype(BF16)
    x_lo = (x - x_hi.astype(F32)).astype(BF16)
    dot = functools.partial(lax.dot_general, dimension_numbers=NT, preferred_element_type=F32)
    total = dot(picked_hi, x_hi) + (dot(picked_hi, x_lo) + dot(picked_lo, x_hi))
    train = jnp.concatenate([total[i * DOC_DEV : (i + 1) * DOC_DEV] for i in range(rows)], axis=1) / counts
    half = train.shape[1] // 2
    out[...] = jnp.concatenate([train[:, :half], train[:, half:]], axis=0).astype(BF16)


def mean_gradients(ids, x_own, g_own, x_sent, g_sent):
    width = g_own.shape[0] * x_own.shape[0]
    return pl.pallas_call(
        train_kernel,
        out_shape=jax.ShapeDtypeStruct((2 * DOC_DEV, width // 2), BF16),
        in_specs=[VMEM] * (4 + len(g_sent)),
        out_specs=VMEM,
        compiler_params=SMALL,
        name="train",
    )(ids, x_own, g_own, x_sent, *g_sent)


def scores_of(trains, queries):
    rows = []
    for train in trains:
        t = train[...].astype(F32)
        rows.append(jnp.concatenate([t[:DOC_DEV], t[DOC_DEV:]], axis=1))
    docs = jnp.concatenate(rows, axis=0).astype(BF16)
    return lax.dot_general(docs, queries[...], NT, preferred_element_type=F32)


def near_kernel(mine, sibling, queries, out):
    width = out.shape[2]
    scores = scores_of((mine, sibling), queries)
    for j in range(out.shape[0]):
        out[j] = scores[:, j * width : (j + 1) * width]


def near_scores(mine, sibling, queries, shares):
    return pl.pallas_call(
        near_kernel,
        out_shape=jax.ShapeDtypeStruct((shares, 2 * DOC_DEV, queries.shape[0] // shares), F32),
        in_specs=[VMEM] * 3,
        out_specs=VMEM,
        compiler_params=SMALL,
        cost_estimate=pl.CostEstimate(flops=3_000_000_000, bytes_accessed=0, transcendentals=0),
        name="near",
    )(mine, sibling, queries)


def score_kernel(flips, mine, sibling, near, *refs):
    blocks, outs = refs[: -len(flips)], refs[-len(flips) :]
    me = lax.axis_index("tensor")
    _, count, width = near.shape
    for i, k in enumerate(flips):
        outs[i][:count, :] = near[me ^ k]
    for m, queries in enumerate(blocks, 1):
        scores = scores_of((mine, sibling), queries)
        for i in range(len(flips)):
            outs[i][m * count : (m + 1) * count, :] = scores[:, i * width : (i + 1) * width]


def score(mine, sibling, near, blocks, flips):
    _, count, width = near.shape
    return pl.pallas_call(
        functools.partial(score_kernel, flips),
        out_shape=[jax.ShapeDtypeStruct((count * (1 + len(blocks)), width), F32)] * len(flips),
        in_specs=[VMEM] * (3 + len(blocks)),
        out_specs=[VMEM] * len(flips),
        compiler_params=SMALL,
        name="score",
    )(mine, sibling, near, *blocks)


def add_kernel(chips, mine, sibling, near, *refs):
    blocks, parts, (kept_own, kept_sum, given) = refs[: chips - 1], refs[chips - 1 : -3], refs[-3:]
    me = lax.axis_index("tensor")
    total = parts[0][...]
    for part in parts[1:]:
        total = total + part[...]
    own = jnp.concatenate([near[me]] + [scores_of((mine, sibling), queries) for queries in blocks], axis=0)
    own = own.reshape(chips, 2, DOC_DEV, total.shape[1])
    summed = total.reshape(chips, 2, DOC_DEV, total.shape[1])
    kept_own[...] = own[:, 0]
    kept_sum[...] = summed[:, 1]
    given[0] = own[:, 1]
    given[1] = summed[:, 0]


def add(mine, sibling, near, blocks, parts):
    chips, width = 1 + len(blocks), near.shape[2]
    shape = (chips, DOC_DEV, width)
    return pl.pallas_call(
        functools.partial(add_kernel, chips),
        out_shape=[jax.ShapeDtypeStruct(s, F32) for s in (shape, shape, (2, *shape))],
        in_specs=[VMEM] * (3 + len(blocks) + len(parts)),
        out_specs=[VMEM] * 3,
        compiler_params=SMALL,
        name="add",
    )(mine, sibling, near, *blocks, *parts)


def place_kernel(kept_own, kept_sum, taken, out):
    me = lax.axis_index("docs")
    for m in range(kept_own.shape[0]):
        out[:, pl.ds(me ^ (2 * m), 1), :] = (kept_own[m] + taken[1, m])[:, None, :]
        out[:, pl.ds(me ^ (2 * m + 1), 1), :] = (kept_sum[m] + taken[0, m])[:, None, :]


def place(kept_own, kept_sum, taken):
    chips, docs, width = kept_own.shape
    return pl.pallas_call(
        place_kernel,
        out_shape=jax.ShapeDtypeStruct((docs, 2 * chips, width), F32),
        in_specs=[VMEM] * 3,
        out_specs=VMEM,
        compiler_params=SMALL,
        name="place",
    )(kept_own, kept_sum, taken)


def per_device(inputs, grads, proj_in, proj_out, queries, ids):
    shares, ndev = lax.axis_size("tensor"), lax.axis_size("docs")
    chips = range(1, ndev // 2)
    flips = list(range(shares - 1, 0, -1))
    x, x_coded, early, late = project_inputs(inputs, proj_in.T, queries, flips)
    flip = shares // 2
    x_sent = swapped(x_coded, "tensor", flip)
    early = [swapped(early, "docs", 2 * m) for m in chips]
    g_own, *g_coded = project_grads(grads, proj_out.T, shares)
    x_sent, g_own = lax.optimization_barrier((x_sent, g_own))
    g_sent = [swapped(g, "tensor", k) for k, g in zip(flips, g_coded)]
    while flip > 1:
        flip //= 2
        x, x_sent = fold_in(x, x_sent)
        x_sent = swapped(x_sent, "tensor", flip)
    mine = mean_gradients(ids, x, g_own, x_sent, g_sent)
    late, mine = lax.optimization_barrier((late, mine))
    late = [swapped(late, "docs", 2 * m) for m in chips]
    sibling = swapped(mine, "docs", 1)
    near = near_scores(mine, sibling, queries, shares)
    scores = score(mine, sibling, near, early, flips)
    arrived = [crossed(s, 1, k) for k, s in zip(flips, scores)]
    kept_own, kept_sum, given = add(mine, sibling, near, late, arrived)
    return place(kept_own, kept_sum, swapped(given, "docs", 1))


def solution(mesh):
    in_specs = (
        P(("group", "docs"), "tensor"),
        P(("group", "docs"), "tensor"),
        P("tensor", None),
        P("tensor", None),
        P(("group", "docs"), "tensor"),
        P(("group", "docs"), None),
    )
    out_specs = P(("group", "docs"), None, "tensor")
    return jax.shard_map(
        per_device, mesh=mesh, in_specs=in_specs, out_specs=out_specs, check_vma=False
    )
```

```python
import functools

import jax
import jax.numpy as jnp
from jax import lax
from jax.experimental import pallas as pl
from jax.experimental.pallas import tpu as pltpu
from jax.sharding import PartitionSpec as P

DOC_DEV = 8
F32 = jnp.float32
BF16 = jnp.bfloat16
NT = (((1,), (1,)), ((), ()))
VMEM = pl.BlockSpec(memory_space=pltpu.VMEM)
ANY = pl.BlockSpec(memory_space=pl.ANY)
STREAM = pltpu.CompilerParams(vmem_limit_bytes=int(53.5 * 2**20))
SMALL = pltpu.CompilerParams(vmem_limit_bytes=8 * 2**20)
STEPS = 32000.0
LANES = 128
MESSAGE_ROWS = 16
ROW_STEPS = 4
X_PIECES, X_AHEAD = 1, 3
G_PIECES, G_AHEAD = 1, 2


def swapped(block, axis, flip):
    return lax.ppermute(block, axis, [(i, i ^ flip) for i in range(lax.axis_size(axis))])


def crossed(block, core, flip):
    shares, ndev = lax.axis_size("tensor"), lax.axis_size("docs")
    pairs = [(d * shares + s, (d ^ core) * shares + (s ^ flip)) for d in range(ndev) for s in range(shares)]
    return lax.ppermute(block, ("docs", "tensor"), pairs)


def coded(v):
    top = jnp.maximum(jnp.max(jnp.abs(v), axis=0, keepdims=True), 1e-30)
    e = jnp.floor(jnp.log2(top)) + 1.0
    steps = jnp.clip(jnp.round(v * (jnp.exp2(-e) * STEPS)), -32767.0, 32767.0)
    return steps.astype(jnp.int32), e.astype(jnp.int32)


def decoded(steps, e):
    return steps.astype(jnp.int32).astype(F32) * (jnp.exp2(e.astype(F32)) * (1.0 / STEPS))


def folded(e):
    return jnp.concatenate([e[:, a : a + LANES] for a in range(0, e.shape[1], LANES)], axis=0)


def unfolded(e):
    return jnp.concatenate([e[a : a + 1] for a in range(e.shape[0])], axis=1)


def write_message(sent, v):
    steps, e = coded(v)
    height, tokens = sent.shape[0], v.shape[1]
    for i, at in enumerate(range(0, v.shape[0], height)):
        sent[:, i * tokens : (i + 1) * tokens] = steps[at : at + height].astype(jnp.int16)
    tail = folded(e)
    if height > tail.shape[0]:
        tail = jnp.concatenate([tail, jnp.zeros((height - tail.shape[0], LANES), jnp.int32)], axis=0)
    sent[:, sent.shape[1] - LANES :] = tail.astype(jnp.int16)


def read_message(sent, tokens):
    last = sent.shape[1] - LANES
    steps = jnp.concatenate([sent[:, at : at + tokens] for at in range(0, last, tokens)], axis=0)
    return decoded(steps, unfolded(sent[:, last:].astype(jnp.int32)[: tokens // LANES]))


def stream_copies(hbm, buffer, sems, pieces):
    rows, columns = buffer.shape[0] // ROW_STEPS, buffer.shape[1] // pieces
    return [
        pltpu.make_async_copy(
            hbm.at[pl.ds(a * rows, rows), pl.ds(c * columns, columns)],
            buffer.at[pl.ds(a * rows, rows), pl.ds(c * columns, columns)],
            sems.at[a * pieces + c],
        )
        for a in range(ROW_STEPS)
        for c in range(pieces)
    ]


def streamed(hbm, weights_hbm, buffer, weights, acc, out, sems, pieces, ahead, between=None):
    me = lax.axis_index("tensor")
    rows, columns = buffer.shape[0] // ROW_STEPS, buffer.shape[1] // pieces
    copies = stream_copies(hbm, buffer, sems, pieces)
    first = pltpu.make_async_copy(weights_hbm, weights, sems.at[len(copies)])
    first.start()
    for copy in copies[:ahead]:
        copy.start()
    if between:
        between(-1)
    first.wait()
    for t, copy in enumerate(copies):
        copy.wait()
        if t + ahead < len(copies):
            copies[t + ahead].start()
        if between:
            between(t)
        a, c = t // pieces, t % pieces

        @pl.when(me >= 0)
        def _():
            d = lax.dot_general(
                buffer[a * rows : (a + 1) * rows, c * columns : (c + 1) * columns],
                weights[:, c * columns : (c + 1) * columns],
                NT,
                preferred_element_type=F32,
            )
            if c > 0:
                d = d + acc[...]
            if c < pieces - 1:
                acc[...] = d
            else:
                out[:, a * rows : (a + 1) * rows] = d.T


def stream_scratch(rows, proj_t, pieces):
    return [
        pltpu.VMEM((rows, proj_t.shape[1]), BF16),
        pltpu.VMEM(proj_t.shape, BF16),
        pltpu.VMEM((rows // ROW_STEPS, proj_t.shape[0]), F32),
        pltpu.SemaphoreType.DMA((ROW_STEPS * pieces + 1,)),
    ]


def inputs_kernel(flips, x_hbm, px_hbm, queries, own, sent, early, late, x, px, acc, sems, staged, cuts):
    me = lax.axis_index("tensor")
    width = late.shape[0]
    staging = pltpu.make_async_copy(queries, staged, cuts.at[len(flips) + 1])
    pieces = [
        pltpu.make_async_copy(
            staged.at[pl.ds(pl.multiple_of((me ^ k) * width, width), width)],
            early.at[pl.ds(i * width, width)] if k else late,
            cuts.at[i],
        )
        for i, k in enumerate(flips + [0])
    ]

    def hand_on(step):
        if step < 0:
            staging.start()
        if step == 2:
            staging.wait()
            for piece in pieces:
                piece.start()

    streamed(x_hbm, px_hbm, x, px, acc, own, sems, X_PIECES, X_AHEAD, hand_on)
    write_message(sent, own[...])
    for piece in pieces:
        piece.wait()


def fold_in_kernel(own, arrived, total, sent):
    v = own[...] + read_message(arrived, own.shape[1])
    total[...] = v
    write_message(sent, v)


def fold_in(own, arrived):
    return pl.pallas_call(
        fold_in_kernel,
        out_shape=[jax.ShapeDtypeStruct(own.shape, F32), jax.ShapeDtypeStruct(arrived.shape, jnp.int16)],
        in_specs=[VMEM] * 2,
        out_specs=[VMEM] * 2,
        compiler_params=SMALL,
        cost_estimate=pl.CostEstimate(flops=20_000_000_000, bytes_accessed=0, transcendentals=0),
        name="fold_in",
    )(own, arrived)


def project_inputs(inputs, proj_t, queries, flips):
    rank, tokens = proj_t.shape[0], inputs.shape[0]
    rows, width = queries.shape[0] // (len(flips) + 1), queries.shape[1]
    return pl.pallas_call(
        functools.partial(inputs_kernel, flips),
        out_shape=[
            jax.ShapeDtypeStruct((rank, tokens), F32),
            jax.ShapeDtypeStruct((MESSAGE_ROWS, rank // MESSAGE_ROWS * tokens + LANES), jnp.int16),
            jax.ShapeDtypeStruct((rows * len(flips), width), BF16),
            jax.ShapeDtypeStruct((rows, width), BF16),
        ],
        in_specs=[ANY] * 3,
        out_specs=[VMEM] * 2 + [ANY] * 2,
        scratch_shapes=stream_scratch(tokens, proj_t, X_PIECES)
        + [pltpu.VMEM(queries.shape, BF16), pltpu.SemaphoreType.DMA((len(flips) + 2,))],
        compiler_params=STREAM,
        name="inputs",
    )(inputs, proj_t, queries)


def grads_kernel(shares, g_hbm, pg_hbm, own, *rest):
    outs, (held, full, g, pg, acc, sems) = rest[: shares - 1], rest[shares - 1 :]
    streamed(g_hbm, pg_hbm, g, pg, acc, full, sems, G_PIECES, G_AHEAD)
    me = lax.axis_index("tensor")
    v = full[...]
    rank, tokens = v.shape
    rows = rank // shares
    steps, e = coded(v)
    tail = folded(e)
    if rows > tail.shape[0]:
        tail = jnp.concatenate([tail, jnp.zeros((rows - tail.shape[0], LANES), jnp.int32)], axis=0)
    tail = tail.astype(jnp.int16)
    held[...] = v.reshape(shares, rows, tokens)
    own[...] = held[me]
    held[...] = steps.astype(F32).reshape(shares, rows, tokens)
    for k, out in enumerate(outs):
        out[:, :tokens] = held[me ^ (len(outs) - k)].astype(jnp.int32).astype(jnp.int16)
        out[:, tokens:] = tail


def project_grads(grads, proj_t, shares):
    rank, tokens = proj_t.shape[0], grads.shape[0]
    rows = rank // shares
    return pl.pallas_call(
        functools.partial(grads_kernel, shares),
        out_shape=[jax.ShapeDtypeStruct((rows, tokens), F32)]
        + [jax.ShapeDtypeStruct((rows, tokens + LANES), jnp.int16)] * (shares - 1),
        in_specs=[ANY] * 2,
        out_specs=[VMEM] * shares,
        scratch_shapes=[pltpu.VMEM((shares, rows, tokens), F32), pltpu.VMEM((rank, tokens), F32)]
        + stream_scratch(tokens, proj_t, G_PIECES),
        compiler_params=pltpu.CompilerParams(vmem_limit_bytes=int(53.5 * 2**20)),
        name="grads",
    )(grads, proj_t)


def train_kernel(ids, x_own, g_own, x_sent, *refs):
    g_sent, out = refs[:-1], refs[-1]
    rank, rows = x_own.shape[0], g_own.shape[0]
    x, g = x_own[...] + read_message(x_sent, g_own.shape[1]), g_own[...]
    for sent in g_sent:
        g = g + read_message(sent, g_own.shape[1])
    tokens = g.shape[1]
    mask = ids[...] == lax.broadcasted_iota(jnp.int32, (DOC_DEV, tokens), 0)
    counts = jnp.sum(mask.astype(F32), axis=1, keepdims=True)
    picked = jnp.concatenate([jnp.where(mask, g[i : i + 1], 0.0) for i in range(rows)], axis=0)
    picked_hi = picked.astype(BF16)
    picked_lo = (picked - picked_hi.astype(F32)).astype(BF16)
    x_hi = x.astype(BF16)
    x_lo = (x - x_hi.astype(F32)).astype(BF16)
    dot = functools.partial(lax.dot_general, dimension_numbers=NT, preferred_element_type=F32)
    total = dot(picked_hi, x_hi) + (dot(picked_hi, x_lo) + dot(picked_lo, x_hi))
    train = jnp.concatenate([total[i * DOC_DEV : (i + 1) * DOC_DEV] for i in range(rows)], axis=1) / counts
    half = train.shape[1] // 2
    out[...] = jnp.concatenate([train[:, :half], train[:, half:]], axis=0).astype(BF16)


def mean_gradients(ids, x_own, g_own, x_sent, g_sent):
    width = g_own.shape[0] * x_own.shape[0]
    return pl.pallas_call(
        train_kernel,
        out_shape=jax.ShapeDtypeStruct((2 * DOC_DEV, width // 2), BF16),
        in_specs=[VMEM] * (4 + len(g_sent)),
        out_specs=VMEM,
        compiler_params=SMALL,
        name="train",
    )(ids, x_own, g_own, x_sent, *g_sent)


def scores_of(trains, queries):
    rows = []
    for train in trains:
        t = train[...].astype(F32)
        rows.append(jnp.concatenate([t[:DOC_DEV], t[DOC_DEV:]], axis=1))
    docs = jnp.concatenate(rows, axis=0).astype(BF16)
    return lax.dot_general(docs, queries[...], NT, preferred_element_type=F32)


def near_kernel(mine, sibling, queries, out):
    width = out.shape[2]
    scores = scores_of((mine, sibling), queries)
    for j in range(out.shape[0]):
        out[j] = scores[:, j * width : (j + 1) * width]


def near_scores(mine, sibling, queries, shares):
    return pl.pallas_call(
        near_kernel,
        out_shape=jax.ShapeDtypeStruct((shares, 2 * DOC_DEV, queries.shape[0] // shares), F32),
        in_specs=[VMEM] * 3,
        out_specs=VMEM,
        compiler_params=SMALL,
        cost_estimate=pl.CostEstimate(flops=3_000_000_000, bytes_accessed=0, transcendentals=0),
        name="near",
    )(mine, sibling, queries)


def score_kernel(flips, mine, sibling, near, *refs):
    blocks, outs = refs[: -len(flips)], refs[-len(flips) :]
    me = lax.axis_index("tensor")
    _, count, width = near.shape
    for i, k in enumerate(flips):
        outs[i][:count, :] = near[me ^ k]
    for m, queries in enumerate(blocks, 1):
        scores = scores_of((mine, sibling), queries)
        for i in range(len(flips)):
            outs[i][m * count : (m + 1) * count, :] = scores[:, i * width : (i + 1) * width]


def score(mine, sibling, near, blocks, flips):
    _, count, width = near.shape
    return pl.pallas_call(
        functools.partial(score_kernel, flips),
        out_shape=[jax.ShapeDtypeStruct((count * (1 + len(blocks)), width), F32)] * len(flips),
        in_specs=[VMEM] * (3 + len(blocks)),
        out_specs=[VMEM] * len(flips),
        compiler_params=SMALL,
        name="score",
    )(mine, sibling, near, *blocks)


def add_kernel(chips, mine, sibling, near, *refs):
    blocks, parts, (kept_own, kept_sum, given) = refs[: chips - 1], refs[chips - 1 : -3], refs[-3:]
    me = lax.axis_index("tensor")
    total = parts[0][...]
    for part in parts[1:]:
        total = total + part[...]
    own = jnp.concatenate([near[me]] + [scores_of((mine, sibling), queries) for queries in blocks], axis=0)
    own = own.reshape(chips, 2, DOC_DEV, total.shape[1])
    summed = total.reshape(chips, 2, DOC_DEV, total.shape[1])
    kept_own[...] = own[:, 0]
    kept_sum[...] = summed[:, 1]
    given[0] = own[:, 1]
    given[1] = summed[:, 0]


def add(mine, sibling, near, blocks, parts):
    chips, width = 1 + len(blocks), near.shape[2]
    shape = (chips, DOC_DEV, width)
    return pl.pallas_call(
        functools.partial(add_kernel, chips),
        out_shape=[jax.ShapeDtypeStruct(s, F32) for s in (shape, shape, (2, *shape))],
        in_specs=[VMEM] * (3 + len(blocks) + len(parts)),
        out_specs=[VMEM] * 3,
        compiler_params=SMALL,
        name="add",
    )(mine, sibling, near, *blocks, *parts)


def place_kernel(kept_own, kept_sum, taken, out):
    me = lax.axis_index("docs")
    for m in range(kept_own.shape[0]):
        out[:, pl.ds(me ^ (2 * m), 1), :] = (kept_own[m] + taken[1, m])[:, None, :]
        out[:, pl.ds(me ^ (2 * m + 1), 1), :] = (kept_sum[m] + taken[0, m])[:, None, :]


def place(kept_own, kept_sum, taken):
    chips, docs, width = kept_own.shape
    return pl.pallas_call(
        place_kernel,
        out_shape=jax.ShapeDtypeStruct((docs, 2 * chips, width), F32),
        in_specs=[VMEM] * 3,
        out_specs=VMEM,
        compiler_params=SMALL,
        name="place",
    )(kept_own, kept_sum, taken)


def per_device(inputs, grads, proj_in, proj_out, queries, ids):
    shares, ndev = lax.axis_size("tensor"), lax.axis_size("docs")
    chips = range(1, ndev // 2)
    flips = list(range(shares - 1, 0, -1))
    x, x_coded, early, late = project_inputs(inputs, proj_in.T, queries, flips)
    flip = shares // 2
    x_sent = swapped(x_coded, "tensor", flip)
    early = [swapped(early, "docs", 2 * m) for m in chips]
    g_own, *g_coded = project_grads(grads, proj_out.T, shares)
    x_sent, g_own = lax.optimization_barrier((x_sent, g_own))
    g_sent = [swapped(g, "tensor", k) for k, g in zip(flips, g_coded)]
    while flip > 1:
        flip //= 2
        x, x_sent = fold_in(x, x_sent)
        x_sent = swapped(x_sent, "tensor", flip)
    mine = mean_gradients(ids, x, g_own, x_sent, g_sent)
    late, mine = lax.optimization_barrier((late, mine))
    late = [swapped(late, "docs", 2 * m) for m in chips]
    sibling = swapped(mine, "docs", 1)
    near = near_scores(mine, sibling, queries, shares)
    scores = score(mine, sibling, near, early, flips)
    arrived = [crossed(s, 1, k) for k, s in zip(flips, scores)]
    kept_own, kept_sum, given = add(mine, sibling, near, late, arrived)
    return place(kept_own, kept_sum, swapped(given, "docs", 1))


def solution(mesh):
    in_specs = (
        P(("group", "docs"), "tensor"),
        P(("group", "docs"), "tensor"),
        P("tensor", None),
        P("tensor", None),
        P(("group", "docs"), "tensor"),
        P(("group", "docs"), None),
    )
    out_specs = P(("group", "docs"), None, "tensor")
    return jax.shard_map(
        per_device, mesh=mesh, in_specs=in_specs, out_specs=out_specs, check_vma=False
    )
```

```python
import functools

import jax
import jax.numpy as jnp
from jax import lax
from jax.experimental import pallas as pl
from jax.experimental.pallas import tpu as pltpu
from jax.sharding import PartitionSpec as P

DOC_DEV = 8
F32 = jnp.float32
BF16 = jnp.bfloat16
NT = (((1,), (1,)), ((), ()))
VMEM = pl.BlockSpec(memory_space=pltpu.VMEM)
ANY = pl.BlockSpec(memory_space=pl.ANY)
STREAM = pltpu.CompilerParams(vmem_limit_bytes=int(53.5 * 2**20))
SMALL = pltpu.CompilerParams(vmem_limit_bytes=8 * 2**20)
STEPS = 32000.0
LANES = 128
MESSAGE_ROWS = 16
ROW_STEPS = 4
X_PIECES, X_AHEAD = 1, 3
G_PIECES, G_AHEAD = 1, 3


def swapped(block, axis, flip):
    return lax.ppermute(block, axis, [(i, i ^ flip) for i in range(lax.axis_size(axis))])


def crossed(block, core, flip):
    shares, ndev = lax.axis_size("tensor"), lax.axis_size("docs")
    pairs = [(d * shares + s, (d ^ core) * shares + (s ^ flip)) for d in range(ndev) for s in range(shares)]
    return lax.ppermute(block, ("docs", "tensor"), pairs)


def coded(v):
    top = jnp.maximum(jnp.max(jnp.abs(v), axis=0, keepdims=True), 1e-30)
    e = jnp.floor(jnp.log2(top)) + 1.0
    steps = jnp.clip(jnp.round(v * (jnp.exp2(-e) * STEPS)), -32767.0, 32767.0)
    return steps.astype(jnp.int32), e.astype(jnp.int32)


def decoded(steps, e):
    return steps.astype(jnp.int32).astype(F32) * (jnp.exp2(e.astype(F32)) * (1.0 / STEPS))


def folded(e):
    return jnp.concatenate([e[:, a : a + LANES] for a in range(0, e.shape[1], LANES)], axis=0)


def unfolded(e):
    return jnp.concatenate([e[a : a + 1] for a in range(e.shape[0])], axis=1)


def write_message(sent, v):
    steps, e = coded(v)
    height, tokens = sent.shape[0], v.shape[1]
    for i, at in enumerate(range(0, v.shape[0], height)):
        sent[:, i * tokens : (i + 1) * tokens] = steps[at : at + height].astype(jnp.int16)
    tail = folded(e)
    if height > tail.shape[0]:
        tail = jnp.concatenate([tail, jnp.zeros((height - tail.shape[0], LANES), jnp.int32)], axis=0)
    sent[:, sent.shape[1] - LANES :] = tail.astype(jnp.int16)


def read_message(sent, tokens):
    last = sent.shape[1] - LANES
    steps = jnp.concatenate([sent[:, at : at + tokens] for at in range(0, last, tokens)], axis=0)
    return decoded(steps, unfolded(sent[:, last:].astype(jnp.int32)[: tokens // LANES]))


def stream_copies(hbm, buffer, sems, pieces):
    rows, columns = buffer.shape[0] // ROW_STEPS, buffer.shape[1] // pieces
    return [
        pltpu.make_async_copy(
            hbm.at[pl.ds(a * rows, rows), pl.ds(c * columns, columns)],
            buffer.at[pl.ds(a * rows, rows), pl.ds(c * columns, columns)],
            sems.at[a * pieces + c],
        )
        for a in range(ROW_STEPS)
        for c in range(pieces)
    ]


def streamed(hbm, weights_hbm, buffer, weights, acc, out, sems, pieces, ahead, between=None):
    me = lax.axis_index("tensor")
    rows, columns = buffer.shape[0] // ROW_STEPS, buffer.shape[1] // pieces
    copies = stream_copies(hbm, buffer, sems, pieces)
    first = pltpu.make_async_copy(weights_hbm, weights, sems.at[len(copies)])
    first.start()
    for copy in copies[:ahead]:
        copy.start()
    if between:
        between(-1)
    first.wait()
    for t, copy in enumerate(copies):
        copy.wait()
        if t + ahead < len(copies):
            copies[t + ahead].start()
        if between:
            between(t)
        a, c = t // pieces, t % pieces

        @pl.when(me >= 0)
        def _():
            d = lax.dot_general(
                buffer[a * rows : (a + 1) * rows, c * columns : (c + 1) * columns],
                weights[:, c * columns : (c + 1) * columns],
                NT,
                preferred_element_type=F32,
            )
            if c > 0:
                d = d + acc[...]
            if c < pieces - 1:
                acc[...] = d
            else:
                out[:, a * rows : (a + 1) * rows] = d.T


def stream_scratch(rows, proj_t, pieces):
    return [
        pltpu.VMEM((rows, proj_t.shape[1]), BF16),
        pltpu.VMEM(proj_t.shape, BF16),
        pltpu.VMEM((rows // ROW_STEPS, proj_t.shape[0]), F32),
        pltpu.SemaphoreType.DMA((ROW_STEPS * pieces + 1,)),
    ]


def inputs_kernel(flips, x_hbm, px_hbm, queries, own, sent, early, late, x, px, acc, sems, staged, cuts):
    me = lax.axis_index("tensor")
    width = late.shape[0]
    staging = pltpu.make_async_copy(queries, staged, cuts.at[len(flips) + 1])
    pieces = [
        pltpu.make_async_copy(
            staged.at[pl.ds(pl.multiple_of((me ^ k) * width, width), width)],
            early.at[pl.ds(i * width, width)] if k else late,
            cuts.at[i],
        )
        for i, k in enumerate(flips + [0])
    ]

    def hand_on(step):
        if step < 0:
            staging.start()
        if step == 2:
            staging.wait()
            for piece in pieces:
                piece.start()

    streamed(x_hbm, px_hbm, x, px, acc, own, sems, X_PIECES, X_AHEAD, hand_on)
    write_message(sent, own[...])
    for piece in pieces:
        piece.wait()


def fold_in_kernel(own, arrived, total, sent):
    v = own[...] + read_message(arrived, own.shape[1])
    total[...] = v
    write_message(sent, v)


def fold_in(own, arrived):
    return pl.pallas_call(
        fold_in_kernel,
        out_shape=[jax.ShapeDtypeStruct(own.shape, F32), jax.ShapeDtypeStruct(arrived.shape, jnp.int16)],
        in_specs=[VMEM] * 2,
        out_specs=[VMEM] * 2,
        compiler_params=SMALL,
        cost_estimate=pl.CostEstimate(flops=20_000_000_000, bytes_accessed=0, transcendentals=0),
        name="fold_in",
    )(own, arrived)


def project_inputs(inputs, proj_t, queries, flips):
    rank, tokens = proj_t.shape[0], inputs.shape[0]
    rows, width = queries.shape[0] // (len(flips) + 1), queries.shape[1]
    return pl.pallas_call(
        functools.partial(inputs_kernel, flips),
        out_shape=[
            jax.ShapeDtypeStruct((rank, tokens), F32),
            jax.ShapeDtypeStruct((MESSAGE_ROWS, rank // MESSAGE_ROWS * tokens + LANES), jnp.int16),
            jax.ShapeDtypeStruct((rows * len(flips), width), BF16),
            jax.ShapeDtypeStruct((rows, width), BF16),
        ],
        in_specs=[ANY] * 3,
        out_specs=[VMEM] * 2 + [ANY] * 2,
        scratch_shapes=stream_scratch(tokens, proj_t, X_PIECES)
        + [pltpu.VMEM(queries.shape, BF16), pltpu.SemaphoreType.DMA((len(flips) + 2,))],
        compiler_params=STREAM,
        name="inputs",
    )(inputs, proj_t, queries)


def grads_kernel(shares, g_hbm, pg_hbm, own, *rest):
    outs, (held, full, g, pg, acc, sems) = rest[: shares - 1], rest[shares - 1 :]
    streamed(g_hbm, pg_hbm, g, pg, acc, full, sems, G_PIECES, G_AHEAD)
    me = lax.axis_index("tensor")
    v = full[...]
    rank, tokens = v.shape
    rows = rank // shares
    steps, e = coded(v)
    tail = folded(e)
    if rows > tail.shape[0]:
        tail = jnp.concatenate([tail, jnp.zeros((rows - tail.shape[0], LANES), jnp.int32)], axis=0)
    tail = tail.astype(jnp.int16)
    held[...] = v.reshape(shares, rows, tokens)
    own[...] = held[me]
    held[...] = steps.astype(F32).reshape(shares, rows, tokens)
    for k, out in enumerate(outs):
        out[:, :tokens] = held[me ^ (len(outs) - k)].astype(jnp.int32).astype(jnp.int16)
        out[:, tokens:] = tail


def project_grads(grads, proj_t, shares):
    rank, tokens = proj_t.shape[0], grads.shape[0]
    rows = rank // shares
    return pl.pallas_call(
        functools.partial(grads_kernel, shares),
        out_shape=[jax.ShapeDtypeStruct((rows, tokens), F32)]
        + [jax.ShapeDtypeStruct((rows, tokens + LANES), jnp.int16)] * (shares - 1),
        in_specs=[ANY] * 2,
        out_specs=[VMEM] * shares,
        scratch_shapes=[pltpu.VMEM((shares, rows, tokens), F32), pltpu.VMEM((rank, tokens), F32)]
        + stream_scratch(tokens, proj_t, G_PIECES),
        compiler_params=pltpu.CompilerParams(vmem_limit_bytes=int(53.5 * 2**20)),
        name="grads",
    )(grads, proj_t)


def train_kernel(ids, x_own, g_own, x_sent, *refs):
    g_sent, out = refs[:-1], refs[-1]
    rank, rows = x_own.shape[0], g_own.shape[0]
    x, g = x_own[...] + read_message(x_sent, g_own.shape[1]), g_own[...]
    for sent in g_sent:
        g = g + read_message(sent, g_own.shape[1])
    tokens = g.shape[1]
    mask = ids[...] == lax.broadcasted_iota(jnp.int32, (DOC_DEV, tokens), 0)
    counts = jnp.sum(mask.astype(F32), axis=1, keepdims=True)
    picked = jnp.concatenate([jnp.where(mask, g[i : i + 1], 0.0) for i in range(rows)], axis=0)
    picked_hi = picked.astype(BF16)
    picked_lo = (picked - picked_hi.astype(F32)).astype(BF16)
    x_hi = x.astype(BF16)
    x_lo = (x - x_hi.astype(F32)).astype(BF16)
    dot = functools.partial(lax.dot_general, dimension_numbers=NT, preferred_element_type=F32)
    total = dot(picked_hi, x_hi) + (dot(picked_hi, x_lo) + dot(picked_lo, x_hi))
    train = jnp.concatenate([total[i * DOC_DEV : (i + 1) * DOC_DEV] for i in range(rows)], axis=1) / counts
    half = train.shape[1] // 2
    out[...] = jnp.concatenate([train[:, :half], train[:, half:]], axis=0).astype(BF16)


def mean_gradients(ids, x_own, g_own, x_sent, g_sent):
    width = g_own.shape[0] * x_own.shape[0]
    return pl.pallas_call(
        train_kernel,
        out_shape=jax.ShapeDtypeStruct((2 * DOC_DEV, width // 2), BF16),
        in_specs=[VMEM] * (4 + len(g_sent)),
        out_specs=VMEM,
        compiler_params=SMALL,
        name="train",
    )(ids, x_own, g_own, x_sent, *g_sent)


def scores_of(trains, queries):
    rows = []
    for train in trains:
        t = train[...].astype(F32)
        rows.append(jnp.concatenate([t[:DOC_DEV], t[DOC_DEV:]], axis=1))
    docs = jnp.concatenate(rows, axis=0).astype(BF16)
    return lax.dot_general(docs, queries, NT, preferred_element_type=F32)


def score_kernel(flip, at, mine, sibling, queries, *refs):
    blocks, out = refs[:-1], refs[-1]
    me = lax.axis_index("tensor")
    count, width = 2 * DOC_DEV, out.shape[1]
    own = queries[pl.ds(pl.multiple_of((me ^ flip) * width, width), width), :]
    rows = [own] + [block[at * width : (at + 1) * width, :] for block in blocks]
    for m, part in enumerate(rows):
        out[m * count : (m + 1) * count, :] = scores_of((mine, sibling), part)


def score(mine, sibling, queries, blocks, flip, at, shares):
    width = queries.shape[0] // shares
    return pl.pallas_call(
        functools.partial(score_kernel, flip, at),
        out_shape=jax.ShapeDtypeStruct((2 * DOC_DEV * (1 + len(blocks)), width), F32),
        in_specs=[VMEM] * (3 + len(blocks)),
        out_specs=VMEM,
        compiler_params=SMALL,
        cost_estimate=pl.CostEstimate(flops=1_000_000_000, bytes_accessed=0, transcendentals=0),
        name="score",
    )(mine, sibling, queries, *blocks)


def add_kernel(chips, own, *refs):
    parts, (kept_own, kept_sum, given) = refs[:-3], refs[-3:]
    total = parts[0][...]
    for part in parts[1:]:
        total = total + part[...]
    mine = own[...].reshape(chips, 2, DOC_DEV, total.shape[1])
    summed = total.reshape(chips, 2, DOC_DEV, total.shape[1])
    kept_own[...] = mine[:, 0]
    kept_sum[...] = summed[:, 1]
    given[0] = mine[:, 1]
    given[1] = summed[:, 0]


def add(own, parts):
    chips, width = own.shape[0] // (2 * DOC_DEV), own.shape[1]
    shape = (chips, DOC_DEV, width)
    return pl.pallas_call(
        functools.partial(add_kernel, chips),
        out_shape=[jax.ShapeDtypeStruct(s, F32) for s in (shape, shape, (2, *shape))],
        in_specs=[VMEM] * (1 + len(parts)),
        out_specs=[VMEM] * 3,
        compiler_params=SMALL,
        name="add",
    )(own, *parts)


def place_kernel(kept_own, kept_sum, taken, out):
    me = lax.axis_index("docs")
    for m in range(kept_own.shape[0]):
        out[:, pl.ds(me ^ (2 * m), 1), :] = (kept_own[m] + taken[1, m])[:, None, :]
        out[:, pl.ds(me ^ (2 * m + 1), 1), :] = (kept_sum[m] + taken[0, m])[:, None, :]


def place(kept_own, kept_sum, taken):
    chips, docs, width = kept_own.shape
    return pl.pallas_call(
        place_kernel,
        out_shape=jax.ShapeDtypeStruct((docs, 2 * chips, width), F32),
        in_specs=[VMEM] * 3,
        out_specs=VMEM,
        compiler_params=SMALL,
        name="place",
    )(kept_own, kept_sum, taken)


def per_device(inputs, grads, proj_in, proj_out, queries, ids):
    shares, ndev = lax.axis_size("tensor"), lax.axis_size("docs")
    chips = range(1, ndev // 2)
    flips = list(range(shares - 1, 0, -1))
    x, x_coded, early, late = project_inputs(inputs, proj_in.T, queries, flips)
    flip = shares // 2
    x_sent = swapped(x_coded, "tensor", flip)
    early = [swapped(early, "docs", 2 * m) for m in chips]
    g_own, *g_coded = project_grads(grads, proj_out.T, shares)
    x_sent, g_own = lax.optimization_barrier((x_sent, g_own))
    g_sent = [swapped(g, "tensor", k) for k, g in zip(flips, g_coded)]
    while flip > 1:
        flip //= 2
        x, x_sent = fold_in(x, x_sent)
        x_sent = swapped(x_sent, "tensor", flip)
    mine = mean_gradients(ids, x, g_own, x_sent, g_sent)
    late, mine = lax.optimization_barrier((late, mine))
    late = [swapped(late, "docs", 2 * m) for m in chips]
    sibling = swapped(mine, "docs", 1)
    arrived = []
    for at, k in enumerate(flips):
        part = score(mine, sibling, queries, early, k, at, shares)
        arrived.append(crossed(part, 1, k))
    own = score(mine, sibling, queries, late, 0, 0, shares)
    kept_own, kept_sum, given = add(own, arrived)
    return place(kept_own, kept_sum, swapped(given, "docs", 1))


def solution(mesh):
    in_specs = (
        P(("group", "docs"), "tensor"),
        P(("group", "docs"), "tensor"),
        P("tensor", None),
        P("tensor", None),
        P(("group", "docs"), "tensor"),
        P(("group", "docs"), None),
    )
    out_specs = P(("group", "docs"), None, "tensor")
    return jax.shard_map(
        per_device, mesh=mesh, in_specs=in_specs, out_specs=out_specs, check_vma=False
    )
```

```python
import functools

import jax
import jax.numpy as jnp
from jax import lax
from jax.experimental import pallas as pl
from jax.experimental.pallas import tpu as pltpu
from jax.sharding import PartitionSpec as P

DOC_DEV = 8
F32 = jnp.float32
BF16 = jnp.bfloat16
NT = (((1,), (1,)), ((), ()))
VMEM = pl.BlockSpec(memory_space=pltpu.VMEM)
ANY = pl.BlockSpec(memory_space=pl.ANY)
STREAM = pltpu.CompilerParams(vmem_limit_bytes=int(53.5 * 2**20))
SMALL = pltpu.CompilerParams(vmem_limit_bytes=8 * 2**20)
STEPS = 32000.0
LANES = 128
MESSAGE_ROWS = 16
ROW_STEPS = 4
X_PIECES, X_AHEAD = 1, 3
G_PIECES, G_AHEAD = 2, 2


def swapped(block, axis, flip):
    return lax.ppermute(block, axis, [(i, i ^ flip) for i in range(lax.axis_size(axis))])


def crossed(block, core, flip):
    shares, ndev = lax.axis_size("tensor"), lax.axis_size("docs")
    pairs = [(d * shares + s, (d ^ core) * shares + (s ^ flip)) for d in range(ndev) for s in range(shares)]
    return lax.ppermute(block, ("docs", "tensor"), pairs)


def coded(v):
    top = jnp.maximum(jnp.max(jnp.abs(v), axis=0, keepdims=True), 1e-30)
    e = jnp.floor(jnp.log2(top)) + 1.0
    steps = jnp.clip(jnp.round(v * (jnp.exp2(-e) * STEPS)), -32767.0, 32767.0)
    return steps.astype(jnp.int32), e.astype(jnp.int32)


def decoded(steps, e):
    return steps.astype(jnp.int32).astype(F32) * (jnp.exp2(e.astype(F32)) * (1.0 / STEPS))


def folded(e):
    return jnp.concatenate([e[:, a : a + LANES] for a in range(0, e.shape[1], LANES)], axis=0)


def unfolded(e):
    return jnp.concatenate([e[a : a + 1] for a in range(e.shape[0])], axis=1)


def write_message(sent, v):
    steps, e = coded(v)
    height, tokens = sent.shape[0], v.shape[1]
    for i, at in enumerate(range(0, v.shape[0], height)):
        sent[:, i * tokens : (i + 1) * tokens] = steps[at : at + height].astype(jnp.int16)
    tail = folded(e)
    if height > tail.shape[0]:
        tail = jnp.concatenate([tail, jnp.zeros((height - tail.shape[0], LANES), jnp.int32)], axis=0)
    sent[:, sent.shape[1] - LANES :] = tail.astype(jnp.int16)


def read_message(sent, tokens):
    last = sent.shape[1] - LANES
    steps = jnp.concatenate([sent[:, at : at + tokens] for at in range(0, last, tokens)], axis=0)
    return decoded(steps, unfolded(sent[:, last:].astype(jnp.int32)[: tokens // LANES]))


def stream_copies(hbm, buffer, sems, pieces, blocks):
    rows, columns = buffer.shape[0] // blocks, buffer.shape[1] // pieces
    return [
        pltpu.make_async_copy(
            hbm.at[pl.ds(a * rows, rows), pl.ds(c * columns, columns)],
            buffer.at[pl.ds(a * rows, rows), pl.ds(c * columns, columns)],
            sems.at[a * pieces + c],
        )
        for a in range(blocks)
        for c in range(pieces)
    ]


def streamed(hbm, weights_hbm, buffer, weights, acc, out, sems, pieces, ahead, between=None):
    me = lax.axis_index("tensor")
    rows, columns = acc.shape[0], buffer.shape[1] // pieces
    copies = stream_copies(hbm, buffer, sems, pieces, buffer.shape[0] // rows)
    first = pltpu.make_async_copy(weights_hbm, weights, sems.at[len(copies)])
    first.start()
    for copy in copies[:ahead]:
        copy.start()
    if between:
        between(-1)
    first.wait()
    for t, copy in enumerate(copies):
        copy.wait()
        if t + ahead < len(copies):
            copies[t + ahead].start()
        if between:
            between(t)
        a, c = t // pieces, t % pieces

        @pl.when(me >= 0)
        def _():
            d = lax.dot_general(
                buffer[a * rows : (a + 1) * rows, c * columns : (c + 1) * columns],
                weights[:, c * columns : (c + 1) * columns],
                NT,
                preferred_element_type=F32,
            )
            if c > 0:
                d = d + acc[...]
            if c < pieces - 1:
                acc[...] = d
            else:
                out[:, a * rows : (a + 1) * rows] = d.T


def stream_scratch(rows, proj_t, pieces, blocks):
    return [
        pltpu.VMEM((rows, proj_t.shape[1]), BF16),
        pltpu.VMEM(proj_t.shape, BF16),
        pltpu.VMEM((rows // blocks, proj_t.shape[0]), F32),
        pltpu.SemaphoreType.DMA((blocks * pieces + 1,)),
    ]


def inputs_kernel(flips, x_hbm, px_hbm, queries, own, sent, early, late, x, px, acc, sems, staged, cuts):
    me = lax.axis_index("tensor")
    width = late.shape[0]
    staging = pltpu.make_async_copy(queries, staged, cuts.at[len(flips) + 1])
    pieces = [
        pltpu.make_async_copy(
            staged.at[pl.ds(pl.multiple_of((me ^ k) * width, width), width)],
            early.at[pl.ds(i * width, width)] if k else late,
            cuts.at[i],
        )
        for i, k in enumerate(flips + [0])
    ]

    def hand_on(step):
        if step < 0:
            staging.start()
        if step == 2:
            staging.wait()
            for piece in pieces:
                piece.start()

    streamed(x_hbm, px_hbm, x, px, acc, own, sems, X_PIECES, X_AHEAD, hand_on)
    write_message(sent, own[...])
    for piece in pieces:
        piece.wait()


def fold_in_kernel(own, arrived, total, sent):
    v = own[...] + read_message(arrived, own.shape[1])
    total[...] = v
    write_message(sent, v)


def fold_in(own, arrived):
    return pl.pallas_call(
        fold_in_kernel,
        out_shape=[jax.ShapeDtypeStruct(own.shape, F32), jax.ShapeDtypeStruct(arrived.shape, jnp.int16)],
        in_specs=[VMEM] * 2,
        out_specs=[VMEM] * 2,
        compiler_params=SMALL,
        cost_estimate=pl.CostEstimate(flops=20_000_000_000, bytes_accessed=0, transcendentals=0),
        name="fold_in",
    )(own, arrived)


def project_inputs(inputs, proj_t, queries, flips):
    rank, tokens = proj_t.shape[0], inputs.shape[0]
    rows, width = queries.shape[0] // (len(flips) + 1), queries.shape[1]
    return pl.pallas_call(
        functools.partial(inputs_kernel, flips),
        out_shape=[
            jax.ShapeDtypeStruct((rank, tokens), F32),
            jax.ShapeDtypeStruct((MESSAGE_ROWS, rank // MESSAGE_ROWS * tokens + LANES), jnp.int16),
            jax.ShapeDtypeStruct((rows * len(flips), width), BF16),
            jax.ShapeDtypeStruct((rows, width), BF16),
        ],
        in_specs=[ANY] * 3,
        out_specs=[VMEM] * 2 + [ANY] * 2,
        scratch_shapes=stream_scratch(tokens, proj_t, X_PIECES, ROW_STEPS)
        + [pltpu.VMEM(queries.shape, BF16), pltpu.SemaphoreType.DMA((len(flips) + 2,))],
        compiler_params=STREAM,
        name="inputs",
    )(inputs, proj_t, queries)


def grads_kernel(shares, g_hbm, pg_hbm, own, *rest):
    outs, (held, full, g, pg, acc, sems) = rest[: shares - 1], rest[shares - 1 :]
    streamed(g_hbm, pg_hbm, g, pg, acc, full, sems, G_PIECES, G_AHEAD)
    me = lax.axis_index("tensor")
    v = full[...]
    rank, tokens = v.shape
    rows = rank // shares
    steps, e = coded(v)
    tail = folded(e)
    if rows > tail.shape[0]:
        tail = jnp.concatenate([tail, jnp.zeros((rows - tail.shape[0], LANES), jnp.int32)], axis=0)
    tail = tail.astype(jnp.int16)
    held[...] = v.reshape(shares, rows, tokens)
    own[...] = held[me]
    held[...] = steps.astype(F32).reshape(shares, rows, tokens)
    for k, out in enumerate(outs):
        out[:, :tokens] = held[me ^ (len(outs) - k)].astype(jnp.int32).astype(jnp.int16)
        out[:, tokens:] = tail


def project_grads(grads, proj_t, shares):
    rank, tokens = proj_t.shape[0], grads.shape[0]
    rows = rank // shares
    return pl.pallas_call(
        functools.partial(grads_kernel, shares),
        out_shape=[jax.ShapeDtypeStruct((rows, tokens), F32)]
        + [jax.ShapeDtypeStruct((rows, tokens + LANES), jnp.int16)] * (shares - 1),
        in_specs=[ANY] * 2,
        out_specs=[VMEM] * shares,
        scratch_shapes=[pltpu.VMEM((shares, rows, tokens), F32), pltpu.VMEM((rank, tokens), F32)]
        + stream_scratch(tokens, proj_t, G_PIECES, ROW_STEPS // 2),
        compiler_params=pltpu.CompilerParams(vmem_limit_bytes=int(53.5 * 2**20)),
        name="grads",
    )(grads, proj_t)


def train_kernel(ids, x_own, g_own, x_sent, *refs):
    g_sent, out = refs[:-1], refs[-1]
    rank, rows = x_own.shape[0], g_own.shape[0]
    x, g = x_own[...] + read_message(x_sent, g_own.shape[1]), g_own[...]
    for sent in g_sent:
        g = g + read_message(sent, g_own.shape[1])
    tokens = g.shape[1]
    mask = ids[...] == lax.broadcasted_iota(jnp.int32, (DOC_DEV, tokens), 0)
    counts = jnp.sum(mask.astype(F32), axis=1, keepdims=True)
    picked = jnp.concatenate([jnp.where(mask, g[i : i + 1], 0.0) for i in range(rows)], axis=0)
    picked_hi = picked.astype(BF16)
    picked_lo = (picked - picked_hi.astype(F32)).astype(BF16)
    x_hi = x.astype(BF16)
    x_lo = (x - x_hi.astype(F32)).astype(BF16)
    dot = functools.partial(lax.dot_general, dimension_numbers=NT, preferred_element_type=F32)
    total = dot(picked_hi, x_hi) + (dot(picked_hi, x_lo) + dot(picked_lo, x_hi))
    train = jnp.concatenate([total[i * DOC_DEV : (i + 1) * DOC_DEV] for i in range(rows)], axis=1) / counts
    half = train.shape[1] // 2
    out[...] = jnp.concatenate([train[:, :half], train[:, half:]], axis=0).astype(BF16)


def mean_gradients(ids, x_own, g_own, x_sent, g_sent):
    width = g_own.shape[0] * x_own.shape[0]
    return pl.pallas_call(
        train_kernel,
        out_shape=jax.ShapeDtypeStruct((2 * DOC_DEV, width // 2), BF16),
        in_specs=[VMEM] * (4 + len(g_sent)),
        out_specs=VMEM,
        compiler_params=SMALL,
        name="train",
    )(ids, x_own, g_own, x_sent, *g_sent)


def scores_of(trains, queries):
    rows = []
    for train in trains:
        t = train[...].astype(F32)
        rows.append(jnp.concatenate([t[:DOC_DEV], t[DOC_DEV:]], axis=1))
    docs = jnp.concatenate(rows, axis=0).astype(BF16)
    return lax.dot_general(docs, queries[...], NT, preferred_element_type=F32)


def near_kernel(mine, sibling, queries, out):
    width = out.shape[2]
    scores = scores_of((mine, sibling), queries)
    for j in range(out.shape[0]):
        out[j] = scores[:, j * width : (j + 1) * width]


def near_scores(mine, sibling, queries, shares):
    return pl.pallas_call(
        near_kernel,
        out_shape=jax.ShapeDtypeStruct((shares, 2 * DOC_DEV, queries.shape[0] // shares), F32),
        in_specs=[VMEM] * 3,
        out_specs=VMEM,
        compiler_params=SMALL,
        cost_estimate=pl.CostEstimate(flops=3_000_000_000, bytes_accessed=0, transcendentals=0),
        name="near",
    )(mine, sibling, queries)


def score_kernel(flips, mine, sibling, near, *refs):
    blocks, outs = refs[: -len(flips)], refs[-len(flips) :]
    me = lax.axis_index("tensor")
    _, count, width = near.shape
    for i, k in enumerate(flips):
        outs[i][:count, :] = near[me ^ k]
    for m, queries in enumerate(blocks, 1):
        scores = scores_of((mine, sibling), queries)
        for i in range(len(flips)):
            outs[i][m * count : (m + 1) * count, :] = scores[:, i * width : (i + 1) * width]


def score(mine, sibling, near, blocks, flips):
    _, count, width = near.shape
    return pl.pallas_call(
        functools.partial(score_kernel, flips),
        out_shape=[jax.ShapeDtypeStruct((count * (1 + len(blocks)), width), F32)] * len(flips),
        in_specs=[VMEM] * (3 + len(blocks)),
        out_specs=[VMEM] * len(flips),
        compiler_params=SMALL,
        name="score",
    )(mine, sibling, near, *blocks)


def add_kernel(chips, mine, sibling, near, *refs):
    blocks, parts, (kept_own, kept_sum, given) = refs[: chips - 1], refs[chips - 1 : -3], refs[-3:]
    me = lax.axis_index("tensor")
    total = parts[0][...]
    for part in parts[1:]:
        total = total + part[...]
    own = jnp.concatenate([near[me]] + [scores_of((mine, sibling), queries) for queries in blocks], axis=0)
    own = own.reshape(chips, 2, DOC_DEV, total.shape[1])
    summed = total.reshape(chips, 2, DOC_DEV, total.shape[1])
    kept_own[...] = own[:, 0]
    kept_sum[...] = summed[:, 1]
    given[0] = own[:, 1]
    given[1] = summed[:, 0]


def add(mine, sibling, near, blocks, parts):
    chips, width = 1 + len(blocks), near.shape[2]
    shape = (chips, DOC_DEV, width)
    return pl.pallas_call(
        functools.partial(add_kernel, chips),
        out_shape=[jax.ShapeDtypeStruct(s, F32) for s in (shape, shape, (2, *shape))],
        in_specs=[VMEM] * (3 + len(blocks) + len(parts)),
        out_specs=[VMEM] * 3,
        compiler_params=SMALL,
        name="add",
    )(mine, sibling, near, *blocks, *parts)


def place_kernel(kept_own, kept_sum, taken, out):
    me = lax.axis_index("docs")
    for m in range(kept_own.shape[0]):
        out[:, pl.ds(me ^ (2 * m), 1), :] = (kept_own[m] + taken[1, m])[:, None, :]
        out[:, pl.ds(me ^ (2 * m + 1), 1), :] = (kept_sum[m] + taken[0, m])[:, None, :]


def place(kept_own, kept_sum, taken):
    chips, docs, width = kept_own.shape
    return pl.pallas_call(
        place_kernel,
        out_shape=jax.ShapeDtypeStruct((docs, 2 * chips, width), F32),
        in_specs=[VMEM] * 3,
        out_specs=VMEM,
        compiler_params=SMALL,
        name="place",
    )(kept_own, kept_sum, taken)


def per_device(inputs, grads, proj_in, proj_out, queries, ids):
    shares, ndev = lax.axis_size("tensor"), lax.axis_size("docs")
    chips = range(1, ndev // 2)
    flips = list(range(shares - 1, 0, -1))
    x, x_coded, early, late = project_inputs(inputs, proj_in.T, queries, flips)
    flip = shares // 2
    x_sent = swapped(x_coded, "tensor", flip)
    early = [swapped(early, "docs", 2 * m) for m in chips]
    g_own, *g_coded = project_grads(grads, proj_out.T, shares)
    x_sent, g_own = lax.optimization_barrier((x_sent, g_own))
    g_sent = [swapped(g, "tensor", k) for k, g in zip(flips, g_coded)]
    while flip > 1:
        flip //= 2
        x, x_sent = fold_in(x, x_sent)
        x_sent = swapped(x_sent, "tensor", flip)
    mine = mean_gradients(ids, x, g_own, x_sent, g_sent)
    late, mine = lax.optimization_barrier((late, mine))
    late = [swapped(late, "docs", 2 * m) for m in chips]
    sibling = swapped(mine, "docs", 1)
    near = near_scores(mine, sibling, queries, shares)
    scores = score(mine, sibling, near, early, flips)
    arrived = [crossed(s, 1, k) for k, s in zip(flips, scores)]
    kept_own, kept_sum, given = add(mine, sibling, near, late, arrived)
    return place(kept_own, kept_sum, swapped(given, "docs", 1))


def solution(mesh):
    in_specs = (
        P(("group", "docs"), "tensor"),
        P(("group", "docs"), "tensor"),
        P("tensor", None),
        P("tensor", None),
        P(("group", "docs"), "tensor"),
        P(("group", "docs"), None),
    )
    out_specs = P(("group", "docs"), None, "tensor")
    return jax.shard_map(
        per_device, mesh=mesh, in_specs=in_specs, out_specs=out_specs, check_vma=False
    )
```
